256 devices in a mesh: wide: 64 (over z, y, core), narrow: 4 (over x).
Axes of the slice: x: 4, y: 4, z: 8, core: 2. Of those that a mesh axis runs over, the one named last changes fastest.
Arguments:
- panel: float32 [131072, 128], P(('wide', 'narrow')), may hold values from -40 to 40
- trailing: float32 [131072, 256], P(('wide', 'narrow')), may hold values from -40 to 40
Outputs:
- q_factor: float32 [131072, 128], P(('wide', 'narrow'))
- r_factor: float32 [128, 128], replicated
- projection: float32 [128, 256], replicated
- updated: float32 [131072, 256], P(('wide', 'narrow'))
The draws below stay inside these ranges and needn't reach their ends.
All inputs are finite; a program needn't handle non-finite values.
Results may differ from the reference program's by a relative error of at most 0.00045.
Values sent between devices are 32-bit elements; how exact they have to be, the bound alone decides.
A program may use at most 64 MiB of HBM per device.

```python
import math
import jax
import jax.numpy as jnp
from jax import lax

PANEL = 128
TRAIL = 256
ROWS = 131072


def design_parts(key):
    keys = jax.random.split(key, 8)
    factor_count = 4
    place = jnp.arange(ROWS, dtype=jnp.float32) / ROWS
    row_base = jnp.exp(jax.random.uniform(keys[0], (ROWS,), jnp.float32, math.log(0.25), math.log(2.5)))
    latent = jnp.clip(jax.random.normal(keys[1], (ROWS, factor_count), jnp.float32), -3.0, 3.0)
    own_noise = jnp.clip(jax.random.normal(keys[2], (ROWS, PANEL), jnp.float32), -4.0, 4.0)
    row_scale = row_base * (0.5 + place)
    raw_loads = jax.random.normal(keys[3], (factor_count, PANEL), jnp.float32)
    loadings = raw_loads / jnp.sum(jnp.abs(raw_loads), axis=0, keepdims=True)
    spread = jnp.exp(jax.random.uniform(keys[6], (PANEL,), jnp.float32, math.log(0.003), math.log(0.03)))
    column_scale = jnp.exp(jax.random.uniform(keys[7], (PANEL,), jnp.float32, math.log(0.3), math.log(3.0)))
    shared = jnp.dot(latent, loadings, precision=lax.Precision.HIGHEST)
    values = shared + own_noise * spread[None, :]
    panel = values * row_scale[:, None] * column_scale[None, :]
    panel = jnp.clip(panel, -40.0, 40.0)
    mixing = jax.random.normal(keys[4], (PANEL, TRAIL), jnp.float32) / math.sqrt(PANEL)
    noise_part = jax.random.normal(keys[5], (ROWS, TRAIL), jnp.float32) * (0.5 + place)[:, None]
    trailing = 0.5 * jnp.dot(panel, mixing, precision=lax.Precision.HIGHEST) + noise_part
    trailing = jnp.clip(trailing, -40.0, 40.0)
    return (panel, trailing)


def draw_panel(key, part):
    return design_parts(jax.random.fold_in(key, 11))[0]


def draw_trailing(key, part):
    return design_parts(jax.random.fold_in(key, 11))[1]


def setup_inputs(seed: int = 0) -> dict:
    key_of = jax.random.split(jax.random.key(seed), 3)
    panel = draw_panel(jax.random.fold_in(key_of[2], 71), 0)
    trailing = draw_trailing(jax.random.fold_in(key_of[2], 71), 0)
    return dict(panel=panel, trailing=trailing)


def upper_factor(gram_matrix):
    order = gram_matrix.shape[0]
    columns = jnp.arange(order, dtype=jnp.int32)

    def column_step(index, state):
        work, factor = state
        where = jnp.asarray(index).astype(jnp.int32)
        pivot_row = lax.dynamic_index_in_dim(work, where, 0, keepdims=False)
        pivot = lax.dynamic_index_in_dim(pivot_row, where, 0, keepdims=False)
        new_row = jnp.where(columns >= where, pivot_row / jnp.sqrt(pivot), jnp.zeros_like(pivot_row))
        work = work - new_row[:, None] * new_row[None, :]
        factor = lax.dynamic_update_slice_in_dim(factor, new_row[None, :], where, 0)
        return (work, factor)
    start = (gram_matrix, jnp.zeros_like(gram_matrix))
    return lax.fori_loop(0, order, column_step, start)[1]

def inverse_upper(upper_part):
    order = upper_part.shape[0]
    identity = jnp.eye(order, dtype=upper_part.dtype)

    def row_step(count, inverse):
        where = (order - 1 - jnp.asarray(count)).astype(jnp.int32)
        upper_row = lax.dynamic_index_in_dim(upper_part, where, 0, keepdims=False)
        unit_row = lax.dynamic_index_in_dim(identity, where, 0, keepdims=False)
        pivot = lax.dynamic_index_in_dim(upper_row, where, 0, keepdims=False)
        partial_value = jnp.dot(upper_row, inverse, precision=lax.Precision.HIGHEST)
        new_row = (unit_row - partial_value) / pivot
        return lax.dynamic_update_slice_in_dim(inverse, new_row[None, :], where, 0)
    return lax.fori_loop(0, order, row_step, jnp.zeros_like(upper_part))

def product(left, right):
    return jnp.dot(left, right, precision=lax.Precision.HIGHEST, preferred_element_type=jnp.float32)

def reference(panel, trailing):
    row_total = jnp.float32(ROWS)
    gram_first = product(panel.T, panel) / row_total
    first_factor = upper_factor(gram_first)
    basis_rows = product(panel, inverse_upper(first_factor))
    gram_second = product(basis_rows.T, basis_rows) / row_total
    second_factor = upper_factor(gram_second)
    q_factor = product(basis_rows, inverse_upper(second_factor))
    r_factor = product(second_factor, first_factor)
    cross_terms = product(panel.T, trailing) / row_total
    projection = product(inverse_upper(r_factor).T, cross_terms)
    updated = trailing - product(q_factor, projection)
    return (q_factor, r_factor, projection, updated)
```

```python
import functools

import jax
import jax.numpy as jnp
from jax import lax
from jax.experimental import pallas as pl
from jax.experimental.pallas import tpu as pltpu
from jax.sharding import PartitionSpec as P

f32 = jnp.float32
bf16 = jnp.bfloat16
HIGHEST = lax.Precision.HIGHEST
MESH = pl.DeviceIdType.MESH

ORDER = 128
TRAIL = 256
NX, NY, NC = 4, 4, 2
SHARES = NX * NY * NC
TILE = 8
WIDTH = 32


def contract(left, right, dims, precision=HIGHEST):
    return lax.dot_general(
        left, right, (dims, ((), ())), precision=precision, preferred_element_type=f32
    )


def two_sum(a, b):
    total = a + b
    part = total - a
    return total, (a - (total - part)) + (b - part)


def slices(values):
    top = jnp.max(jnp.abs(values), axis=0, keepdims=True)
    unit = (top + top * (2.0**-23)) - top
    shift = unit * (1.5 * 2.0**40)
    parts = []
    rest = values
    for _ in range(3):
        part = (rest + shift) - shift
        rest = rest - part
        shift = shift * (2.0**-8)
        parts.append(part.astype(bf16))
    parts.append(rest.astype(bf16))
    return parts


def gram_parts(parts):
    first = contract(parts[0], jnp.concatenate(parts, axis=1), ((0,), (0,)), None)
    second = contract(parts[1], jnp.concatenate(parts[1:], axis=1), ((0,), (0,)), None)
    third = contract(parts[2], parts[2], ((0,), (0,)), None)
    n = ORDER
    cross = first[:, n : 2 * n]
    tail = (first[:, 2 * n : 3 * n] + second[:, n : 2 * n]) + (
        first[:, 3 * n :] + second[:, 2 * n :]
    )
    return first[:, :n], cross + cross.T, (tail + tail.T) + (second[:, :n] + third)


def factor(work):
    order, width = work.shape[0], WIDTH
    rows = lax.broadcasted_iota(jnp.int32, (order, order), 0)
    cols = lax.broadcasted_iota(jnp.int32, (order, order), 1)
    inverse = jnp.where(rows == cols, 1.0, 0.0).astype(f32)
    sub = lax.broadcasted_iota(jnp.int32, (width, order), 0)
    lane = lax.broadcasted_iota(jnp.int32, (width, order), 1)
    uppers, inverses = [], []
    for start in range(0, order, width):
        top, top_inverse = work[:width], inverse[:width]
        column = jnp.stack(
            [
                jnp.broadcast_to(top[:, start + k : start + k + 1], (width, order))
                for k in range(width)
            ]
        )
        pivots = jnp.ones((width, order), f32)
        for i in range(width):
            pivot = column[0, i : i + 1, :]
            pivots = jnp.where(sub == i, pivot, pivots)
            if i + 1 < width:
                ratio = jnp.where(sub > i, column[0] * (1.0 / pivot), 0.0)
                column = column[1:] - ratio[None] * column[1:, i : i + 1, :]
                top = top - ratio * top[i : i + 1, :]
                top_inverse = top_inverse - ratio * top_inverse[i : i + 1, :]
        scale = lax.rsqrt(pivots)
        upper = jnp.where(sub + start <= lane, top * scale, 0.0)
        lower = top_inverse * scale
        uppers.append(upper)
        inverses.append(lower)
        if start + width < order:
            both = jnp.concatenate([upper, lower], axis=1)
            step = contract(upper, both, ((0,), (0,)))[start + width :]
            work = work[width:] - step[:, :order]
            inverse = inverse[width:] - step[:, order:]
    return jnp.concatenate(uppers, axis=0), jnp.concatenate(inverses, axis=0)


def swap(tiles):
    return pltpu.roll(tiles, 4, tiles.ndim - 2)


def halves(left, right):
    left = left.reshape(ORDER // TILE, TILE, ORDER)
    right = swap(right.reshape(ORDER // TILE, TILE, ORDER))
    low = lax.broadcasted_iota(jnp.int32, left.shape, 1) < 4
    return jnp.where(low, left, right), jnp.where(low, right, left)


def unhalve(even, odd):
    low = lax.broadcasted_iota(jnp.int32, even.shape, 1) < 4
    left = jnp.where(low, even, odd)
    right = swap(jnp.where(low, odd, even))
    return left.reshape(ORDER, ORDER), right.reshape(ORDER, ORDER)


def add_up(terms, core):
    sub = lax.broadcasted_iota(jnp.int32, (TILE, ORDER), 0)
    mine = (sub // 4) == core
    total, error = terms[0][:TILE], jnp.zeros((TILE, ORDER), f32)
    plain = [t[TILE:] for t in terms]
    for term in terms[1:]:
        total, more = two_sum(total, term[:TILE])
        error = error + more
    low = error + swap(total + error)
    high = total + low
    rest = low - (high - total)
    while len(plain) > 1:
        plain = [a + b for a, b in zip(plain[::2], plain[1::2])] + (
            [plain[-1]] if len(plain) % 2 else []
        )
    return jnp.where(mine, high, swap(rest)), plain[0]


def reduce_kernel(
    nz, row_total,
    panel_ref, trail_ref, high_ref, low_ref, cross_ref,
    panel, trail, send, rs_in, z_out, z_in, gathered,
    load_sem, rs_send, rs_recv, z_send, z_recv, ag_send, ag_recv,
):
    load_panel = pltpu.make_async_copy(panel_ref, panel, load_sem.at[0])
    load_trail = pltpu.make_async_copy(trail_ref, trail, load_sem.at[1])
    load_panel.start()
    load_trail.start()

    wide, x = lax.axis_index("wide"), lax.axis_index("narrow")
    z, y, core = wide // (NY * NC), (wide // NC) % NY, wide % NC
    share = (x * NY + y) * NC + core

    near = []
    for dx in range(NX):
        for dy in range(NY):
            for dc in range(NC):
                if dx or dy or dc:
                    hops = min(dx, NX - dx) + min(dy, NY - dy)
                    near.append((-hops, dx, dy, dc))
    near = sorted(near)

    def neighbour(dx, dy, dc):
        px, py, pc = (x + dx) % NX, (y + dy) % NY, (core + dc) % NC
        return (px * NY + py) * NC + pc, ((z * NY + py) * NC + pc, px)

    around = [neighbour(dx, dy, dc) for _, dx, dy, dc in near]
    steps = sorted(range(1, nz), key=lambda d: -min(d, nz - d))
    along = [((((z + d) % nz) * NY + y) * NC + core, x) for d in steps]

    barrier = pltpu.get_barrier_semaphore()
    for device in along + [device for _, device in around]:
        pl.semaphore_signal(barrier, inc=1, device_id=device, device_id_type=MESH)

    load_panel.wait()
    scale = 1.0 / row_total
    parts = slices(panel[...])
    lead, second, third = gram_parts(parts)
    high, error = two_sum(lead, second)
    error = error + third
    total = high + error
    error = error - (total - high)
    even, odd = halves(total * scale, error * scale)
    send[:, 0, :TILE, :] = even
    send[:, 1, :TILE, :] = odd

    load_trail.wait()
    values = trail[...]
    t0 = values.astype(bf16)
    values = values - t0.astype(f32)
    t1 = values.astype(bf16)
    t2 = (values - t1.astype(f32)).astype(bf16)
    tn = ((0,), (0,))
    both = contract(parts[0], jnp.concatenate([t0, t1, t2], axis=1), tn, None)
    more = contract(parts[1], jnp.concatenate([t0, t1], axis=1), tn, None)
    last = contract(parts[2], t0, tn, None)
    cross = both[:, :TRAIL] + (
        (both[:, TRAIL : 2 * TRAIL] + more[:, :TRAIL])
        + (both[:, 2 * TRAIL :] + more[:, TRAIL:] + last)
    )
    cross = cross * scale
    even, odd = halves(cross[:, :ORDER], cross[:, ORDER:])
    send[:, 0, TILE:, :] = even
    send[:, 1, TILE:, :] = odd

    pl.semaphore_wait(barrier, len(along) + len(around))

    for slot, (target, device) in enumerate(around):
        pltpu.make_async_remote_copy(
            src_ref=send.at[target // NC, target % NC],
            dst_ref=rs_in.at[slot],
            send_sem=rs_send,
            recv_sem=rs_recv,
            device_id=device,
            device_id_type=MESH,
        ).start()
    pltpu.make_async_copy(rs_in, rs_in, rs_recv).wait()
    terms = [send[share // NC, share % NC]] + [rs_in[k] for k in range(SHARES - 1)]
    pair, plain = add_up(terms, core)
    z_out[:TILE] = pair
    z_out[TILE:] = plain

    for device in along:
        pltpu.make_async_remote_copy(
            src_ref=z_out,
            dst_ref=z_in.at[z],
            send_sem=z_send,
            recv_sem=z_recv,
            device_id=device,
            device_id_type=MESH,
        ).start()
    z_in[z] = z_out[...]
    pltpu.make_async_copy(z_in.at[pl.ds(0, nz - 1)], z_in.at[pl.ds(0, nz - 1)], z_recv).wait()
    pair, plain = add_up([z_in[k] for k in range(nz)], core)
    gathered[share, :TILE] = pair
    gathered[share, TILE:] = plain

    for _, device in around:
        pltpu.make_async_remote_copy(
            src_ref=gathered.at[share],
            dst_ref=gathered.at[share],
            send_sem=ag_send,
            recv_sem=ag_recv,
            device_id=device,
            device_id_type=MESH,
        ).start()
    some = gathered.at[pl.ds(0, SHARES - 1)]
    pltpu.make_async_copy(some, some, ag_recv).wait()

    blocks = gathered[...].reshape(SHARES // 2, 2, 2 * TILE, ORDER)
    high, low = unhalve(blocks[:, 0, :TILE], blocks[:, 1, :TILE])
    high_ref[...] = high
    low_ref[...] = low
    left, right = unhalve(blocks[:, 0, TILE:], blocks[:, 1, TILE:])
    cross_ref[:, :ORDER] = left
    cross_ref[:, ORDER:] = right

    pltpu.make_async_copy(rs_in, rs_in, rs_send).wait()
    pltpu.make_async_copy(z_in.at[pl.ds(0, nz - 1)], z_in.at[pl.ds(0, nz - 1)], z_send).wait()
    pltpu.make_async_copy(some, some, ag_send).wait()


def reduced(panel, trailing, nz, row_total):
    rows = panel.shape[0]
    block = (2 * TILE, ORDER)
    vmem = pl.BlockSpec(memory_space=pltpu.VMEM)
    square = jax.ShapeDtypeStruct((ORDER, ORDER), f32)
    dma = pltpu.SemaphoreType.DMA
    return pl.pallas_call(
        functools.partial(reduce_kernel, nz, row_total),
        out_shape=[square, square, jax.ShapeDtypeStruct((ORDER, TRAIL), f32)],
        in_specs=[pl.BlockSpec(memory_space=pltpu.HBM)] * 2,
        out_specs=[vmem] * 3,
        scratch_shapes=[
            pltpu.VMEM((rows, ORDER), f32),
            pltpu.VMEM((rows, TRAIL), f32),
            pltpu.VMEM((SHARES // 2, 2) + block, f32),
            pltpu.VMEM((SHARES - 1,) + block, f32),
            pltpu.VMEM(block, f32),
            pltpu.VMEM((nz,) + block, f32),
            pltpu.VMEM((SHARES,) + block, f32),
            dma((2,)),
            dma, dma, dma, dma, dma, dma,
        ],
        compiler_params=pltpu.CompilerParams(
            collective_id=0, has_side_effects=True, vmem_limit_bytes=62 * 2**20
        ),
        name="reduce_grams",
    )(panel, trailing)


def apply_kernel(
    high_ref, low_ref, cross_ref, panel_ref, trail_ref, q_ref, r_ref, p_ref, u_ref,
    panel, trail, q_out, u_out, load_sem, store_sem,
):
    load_panel = pltpu.make_async_copy(panel_ref, panel, load_sem.at[0])
    load_trail = pltpu.make_async_copy(trail_ref, trail, load_sem.at[1])
    load_panel.start()
    load_trail.start()
    nn, nt = ((1,), (0,)), ((1,), (1,))
    high = high_ref[...]
    first_factor, first_inverse = factor(high)
    lead, second, third = gram_parts(slices(first_factor))
    rest, error = two_sum(high, -lead)
    rest, more = two_sum(rest, -second)
    gap = rest + ((error + more) + (low_ref[...] - third))
    eye = lax.broadcasted_iota(jnp.int32, gap.shape, 0) == lax.broadcasted_iota(
        jnp.int32, gap.shape, 1
    )
    eye = jnp.where(eye, 1.0, 0.0).astype(f32)
    gap = contract(contract(first_inverse, gap, nn), first_inverse, nt)
    gram_second = eye + gap
    second_factor, second_inverse = factor(gram_second)
    r_factor = contract(second_factor, first_factor, nn)
    r_ref[...] = r_factor
    inverse = contract(second_inverse, first_inverse, nn)
    inverse = inverse + contract(eye - contract(inverse, r_factor, nt), inverse, nn)
    projection = contract(inverse, cross_ref[...], nn)
    p_ref[...] = projection
    load_panel.wait()
    q_factor = contract(panel[...], inverse, nt)
    q_out[...] = q_factor
    store_q = pltpu.make_async_copy(q_out, q_ref, store_sem.at[0])
    store_q.start()
    load_trail.wait()
    u_out[...] = trail[...] - contract(q_factor, projection, nn)
    store_u = pltpu.make_async_copy(u_out, u_ref, store_sem.at[1])
    store_u.start()
    store_q.wait()
    store_u.wait()


def applied(high, low, cross, panel, trailing):
    rows = panel.shape[0]
    vmem = pl.BlockSpec(memory_space=pltpu.VMEM)
    hbm = pl.BlockSpec(memory_space=pltpu.HBM)
    dma = pltpu.SemaphoreType.DMA
    return pl.pallas_call(
        apply_kernel,
        out_shape=[
            jax.ShapeDtypeStruct((rows, ORDER), f32),
            jax.ShapeDtypeStruct((ORDER, ORDER), f32),
            jax.ShapeDtypeStruct((ORDER, TRAIL), f32),
            jax.ShapeDtypeStruct((rows, TRAIL), f32),
        ],
        in_specs=[vmem] * 3 + [hbm] * 2,
        out_specs=[hbm, vmem, vmem, hbm],
        scratch_shapes=[
            pltpu.VMEM((rows, ORDER), f32),
            pltpu.VMEM((rows, TRAIL), f32),
            pltpu.VMEM((rows, ORDER), f32),
            pltpu.VMEM((rows, TRAIL), f32),
            dma((2,)),
            dma((2,)),
        ],
        compiler_params=pltpu.CompilerParams(vmem_limit_bytes=62 * 2**20),
        name="factor_and_apply",
    )(high, low, cross, panel, trailing)


def solution(mesh):
    nz = mesh.shape["wide"] // (NY * NC)

    def on_device(panel, trailing):
        row_total = float(panel.shape[0] * mesh.size)
        high, low, cross = reduced(panel, trailing, nz, row_total)
        q_factor, r_factor, projection, updated = applied(high, low, cross, panel, trailing)
        return q_factor, r_factor, projection, updated

    rows = P(("wide", "narrow"), None)
    return jax.shard_map(
        on_device, mesh=mesh, in_specs=(rows, rows), out_specs=(rows, P(), P(), rows),
        check_vma=False,
    )
```

```python
import functools

import jax
import jax.numpy as jnp
from jax import lax
from jax.experimental import pallas as pl
from jax.experimental.pallas import tpu as pltpu
from jax.sharding import PartitionSpec as P

f32 = jnp.float32
bf16 = jnp.bfloat16
HIGHEST = lax.Precision.HIGHEST
MESH = pl.DeviceIdType.MESH

ORDER = 128
TRAIL = 256
NX, NY, NC = 4, 4, 2
SHARES = NX * NY * NC
TILE = 8
WIDTH = 32


def contract(left, right, dims, precision=HIGHEST):
    return lax.dot_general(
        left, right, (dims, ((), ())), precision=precision, preferred_element_type=f32
    )


def two_sum(a, b):
    total = a + b
    part = total - a
    return total, (a - (total - part)) + (b - part)


def slices(values):
    top = jnp.max(jnp.abs(values), axis=0, keepdims=True)
    unit = (top + top * (2.0**-23)) - top
    shift = unit * (1.5 * 2.0**40)
    parts = []
    rest = values
    for _ in range(3):
        part = (rest + shift) - shift
        rest = rest - part
        shift = shift * (2.0**-8)
        parts.append(part.astype(bf16))
    parts.append(rest.astype(bf16))
    return parts


def gram_parts(parts):
    first = contract(parts[0], jnp.concatenate(parts, axis=1), ((0,), (0,)), None)
    second = contract(parts[1], jnp.concatenate(parts[1:], axis=1), ((0,), (0,)), None)
    third = contract(parts[2], parts[2], ((0,), (0,)), None)
    n = ORDER
    cross = first[:, n : 2 * n]
    tail = (first[:, 2 * n : 3 * n] + second[:, n : 2 * n]) + (
        first[:, 3 * n :] + second[:, 2 * n :]
    )
    return first[:, :n], cross + cross.T, (tail + tail.T) + (second[:, :n] + third)


def factor(work):
    order, width = work.shape[0], WIDTH
    rows = lax.broadcasted_iota(jnp.int32, (order, order), 0)
    cols = lax.broadcasted_iota(jnp.int32, (order, order), 1)
    inverse = jnp.where(rows == cols, 1.0, 0.0).astype(f32)
    sub = lax.broadcasted_iota(jnp.int32, (width, order), 0)
    lane = lax.broadcasted_iota(jnp.int32, (width, order), 1)
    uppers, inverses = [], []
    for start in range(0, order, width):
        top, top_inverse = work[:width], inverse[:width]
        column = jnp.stack(
            [
                jnp.broadcast_to(top[:, start + k : start + k + 1], (width, order))
                for k in range(width)
            ]
        )
        pivots = jnp.ones((width, order), f32)
        for i in range(width):
            pivot = column[0, i : i + 1, :]
            pivots = jnp.where(sub == i, pivot, pivots)
            if i + 1 < width:
                ratio = jnp.where(sub > i, column[0], 0.0) * (1.0 / pivot)
                column = column[1:] - ratio[None] * column[1:, i : i + 1, :]
                top = top - ratio * top[i : i + 1, :]
                top_inverse = top_inverse - ratio * top_inverse[i : i + 1, :]
        scale = lax.rsqrt(pivots)
        upper = jnp.where(sub + start <= lane, top * scale, 0.0)
        lower = top_inverse * scale
        uppers.append(upper)
        inverses.append(lower)
        if start + width < order:
            both = jnp.concatenate([upper, lower], axis=1)
            step = contract(upper, both, ((0,), (0,)))[start + width :]
            work = work[width:] - step[:, :order]
            inverse = inverse[width:] - step[:, order:]
    return jnp.concatenate(uppers, axis=0), jnp.concatenate(inverses, axis=0)


def swap(tiles):
    return pltpu.roll(tiles, 4, tiles.ndim - 2)


def halves(left, right):
    left = left.reshape(ORDER // TILE, TILE, ORDER)
    right = swap(right.reshape(ORDER // TILE, TILE, ORDER))
    low = lax.broadcasted_iota(jnp.int32, left.shape, 1) < 4
    return jnp.where(low, left, right), jnp.where(low, right, left)


def unhalve(even, odd):
    low = lax.broadcasted_iota(jnp.int32, even.shape, 1) < 4
    left = jnp.where(low, even, odd)
    right = swap(jnp.where(low, odd, even))
    return left.reshape(ORDER, ORDER), right.reshape(ORDER, ORDER)


def add_pairs(terms, core):
    sub = lax.broadcasted_iota(jnp.int32, (TILE, ORDER), 0)
    mine = (sub // 4) == core
    total, error = terms[0], jnp.zeros((TILE, ORDER), f32)
    for term in terms[1:]:
        total, more = two_sum(total, term)
        error = error + more
    low = error + swap(total + error)
    high = total + low
    return jnp.where(mine, high, swap(low - (high - total)))


def add_plain(terms):
    while len(terms) > 1:
        terms = [a + b for a, b in zip(terms[::2], terms[1::2])] + (
            [terms[-1]] if len(terms) % 2 else []
        )
    return terms[0]


def reduce_kernel(
    nz, row_total,
    panel_ref, trail_ref, factor_ref, inverse_ref, gap_ref, cross_ref,
    panel, trail, send, rs_in, z_out, z_in, gathered,
    load_sem, rs_send, rs_recv, z_send, z_recv, ag_send, ag_recv,
):
    load_panel = pltpu.make_async_copy(panel_ref, panel, load_sem.at[0])
    load_trail = pltpu.make_async_copy(trail_ref, trail, load_sem.at[1])
    load_panel.start()
    load_trail.start()

    wide, x = lax.axis_index("wide"), lax.axis_index("narrow")
    z, y, core = wide // (NY * NC), (wide // NC) % NY, wide % NC
    share = (x * NY + y) * NC + core

    near = []
    for dx in range(NX):
        for dy in range(NY):
            for dc in range(NC):
                if dx or dy or dc:
                    hops = min(dx, NX - dx) + min(dy, NY - dy)
                    near.append((-hops, dx, dy, dc))
    near = sorted(near)

    def neighbour(dx, dy, dc):
        px, py, pc = (x + dx) % NX, (y + dy) % NY, (core + dc) % NC
        return (px * NY + py) * NC + pc, ((z * NY + py) * NC + pc, px)

    around = [neighbour(dx, dy, dc) for _, dx, dy, dc in near]
    steps = sorted(range(1, nz), key=lambda d: -min(d, nz - d))
    along = [((((z + d) % nz) * NY + y) * NC + core, x) for d in steps]

    barrier = pltpu.get_barrier_semaphore()
    for device in along + [device for _, device in around]:
        pl.semaphore_signal(barrier, inc=1, device_id=device, device_id_type=MESH)

    def copy(src, dst, send_sem, recv_sem, device):
        pltpu.make_async_remote_copy(
            src_ref=src, dst_ref=dst, send_sem=send_sem, recv_sem=recv_sem,
            device_id=device, device_id_type=MESH,
        ).start()

    def scatter(k):
        for slot, (target, device) in enumerate(around):
            copy(
                send.at[k, target // NC, target % NC], rs_in.at[k, slot],
                rs_send.at[k], rs_recv.at[k], device,
            )

    def scattered(k):
        pltpu.make_async_copy(rs_in.at[k], rs_in.at[k], rs_recv.at[k]).wait()
        return [send[k, share // NC, share % NC]] + [rs_in[k, n] for n in range(SHARES - 1)]

    def exchange(k, block):
        z_out[k] = block
        for device in along:
            copy(z_out.at[k], z_in.at[k, z], z_send.at[k], z_recv.at[k], device)
        z_in[k, z] = block

    def exchanged(k):
        others = z_in.at[k, pl.ds(0, nz - 1)]
        pltpu.make_async_copy(others, others, z_recv.at[k]).wait()
        return [z_in[k, n] for n in range(nz)]

    def gather(k, block):
        gathered[k, share] = block
        for _, device in around:
            copy(
                gathered.at[k, share], gathered.at[k, share],
                ag_send.at[k], ag_recv.at[k], device,
            )

    def gathered_pair(k):
        others = gathered.at[k, pl.ds(0, SHARES - 1)]
        pltpu.make_async_copy(others, others, ag_recv.at[k]).wait()
        blocks = gathered[k].reshape(SHARES // NC, NC, TILE, ORDER)
        return unhalve(blocks[:, 0], blocks[:, 1])

    def stage(k, left, right):
        even, odd = halves(left, right)
        send[k, :, 0] = even
        send[k, :, 1] = odd

    load_panel.wait()
    scale = 1.0 / row_total
    parts = slices(panel[...])
    lead, second, third = gram_parts(parts)
    high, error = two_sum(lead, second)
    error = error + third
    total = high + error
    error = error - (total - high)
    stage(0, total * scale, error * scale)

    pl.semaphore_wait(barrier, len(along) + len(around))
    scatter(0)

    load_trail.wait()
    values = trail[...]
    t0 = values.astype(bf16)
    values = values - t0.astype(f32)
    t1 = values.astype(bf16)
    t2 = (values - t1.astype(f32)).astype(bf16)
    tn = ((0,), (0,))
    both = contract(parts[0], jnp.concatenate([t0, t1, t2], axis=1), tn, None)
    more = contract(parts[1], jnp.concatenate([t0, t1], axis=1), tn, None)
    last = contract(parts[2], t0, tn, None)
    cross = both[:, :TRAIL] + (
        (both[:, TRAIL : 2 * TRAIL] + more[:, :TRAIL])
        + (both[:, 2 * TRAIL :] + more[:, TRAIL:] + last)
    )
    cross = cross * scale
    stage(1, cross[:, :ORDER], cross[:, ORDER:])
    scatter(1)

    exchange(0, add_pairs(scattered(0), core))
    exchange(1, add_plain(scattered(1)))
    gather(0, add_pairs(exchanged(0), core))
    gather(1, add_plain(exchanged(1)))
    high, low = gathered_pair(0)

    nn, nt = ((1,), (0,)), ((1,), (1,))
    first_factor, first_inverse = factor(high)
    factor_ref[...] = first_factor
    inverse_ref[...] = first_inverse
    lead, second, third = gram_parts(slices(first_factor))
    rest, error = two_sum(high, -lead)
    rest, more = two_sum(rest, -second)
    gap = rest + ((error + more) + (low - third))
    gap_ref[...] = contract(contract(first_inverse, gap, nn), first_inverse, nt)

    left, right = gathered_pair(1)
    cross_ref[:, :ORDER] = left
    cross_ref[:, ORDER:] = right

    for k in range(2):
        pltpu.make_async_copy(rs_in.at[k], rs_in.at[k], rs_send.at[k]).wait()
        others = z_in.at[k, pl.ds(0, nz - 1)]
        pltpu.make_async_copy(others, others, z_send.at[k]).wait()
        others = gathered.at[k, pl.ds(0, SHARES - 1)]
        pltpu.make_async_copy(others, others, ag_send.at[k]).wait()


def reduced(panel, trailing, nz, row_total):
    rows = panel.shape[0]
    block = (TILE, ORDER)
    vmem = pl.BlockSpec(memory_space=pltpu.VMEM)
    square = jax.ShapeDtypeStruct((ORDER, ORDER), f32)
    dma = pltpu.SemaphoreType.DMA
    return pl.pallas_call(
        functools.partial(reduce_kernel, nz, row_total),
        out_shape=[square, square, square, jax.ShapeDtypeStruct((ORDER, TRAIL), f32)],
        in_specs=[pl.BlockSpec(memory_space=pltpu.HBM)] * 2,
        out_specs=[vmem] * 4,
        scratch_shapes=[
            pltpu.VMEM((rows, ORDER), f32),
            pltpu.VMEM((rows, TRAIL), f32),
            pltpu.VMEM((2, SHARES // NC, NC) + block, f32),
            pltpu.VMEM((2, SHARES - 1) + block, f32),
            pltpu.VMEM((2,) + block, f32),
            pltpu.VMEM((2, nz) + block, f32),
            pltpu.VMEM((2, SHARES) + block, f32),
        ]
        + [dma((2,))] * 7,
        compiler_params=pltpu.CompilerParams(
            collective_id=0, has_side_effects=True, vmem_limit_bytes=62 * 2**20
        ),
        name="reduce_and_factor",
    )(panel, trailing)


def apply_kernel(
    factor_ref, inverse_ref, gap_ref, cross_ref, panel_ref, trail_ref,
    q_ref, r_ref, p_ref, u_ref,
    panel, trail, q_out, u_out, whole, load_sem, store_sem,
):
    load_panel = pltpu.make_async_copy(panel_ref, panel, load_sem.at[0])
    load_trail = pltpu.make_async_copy(trail_ref, trail, load_sem.at[1])
    load_panel.start()
    load_trail.start()
    nn, nt, tn = ((1,), (0,)), ((1,), (1,)), ((0,), (0,))
    gap = gap_ref[...]
    rows = lax.broadcasted_iota(jnp.int32, gap.shape, 0)
    cols = lax.broadcasted_iota(jnp.int32, gap.shape, 1)
    eye = jnp.where(rows == cols, 1.0, 0.0).astype(f32)
    weight = jnp.where(rows < cols, 1.0, 0.5 * eye).astype(f32)
    small = jnp.sum(gap * gap) < 2.0**-7

    @pl.when(small)
    def _():
        first_factor, first_inverse, gap = factor_ref[...], inverse_ref[...], gap_ref[...]
        upper = weight * gap
        for _ in range(5):
            upper = weight * (gap - contract(upper, upper, tn))
        r_ref[...] = first_factor + contract(upper, first_factor, nn)
        once = first_inverse - contract(upper, first_inverse, tn)
        whole[...] = first_inverse - contract(upper, once, tn)

    @pl.when(jnp.logical_not(small))
    def _():
        second_factor, second_inverse = factor(eye + gap_ref[...])
        r_ref[...] = contract(second_factor, factor_ref[...], nn)
        whole[...] = contract(second_inverse, inverse_ref[...], nn)

    inverse = whole[...]
    inverse = inverse + contract(eye - contract(inverse, r_ref[...], nt), inverse, nn)
    projection = contract(inverse, cross_ref[...], nn)
    p_ref[...] = projection
    load_panel.wait()
    q_factor = contract(panel[...], inverse, nt)
    q_out[...] = q_factor
    store_q = pltpu.make_async_copy(q_out, q_ref, store_sem.at[0])
    store_q.start()
    load_trail.wait()
    u_out[...] = trail[...] - contract(q_factor, projection, nn)
    store_u = pltpu.make_async_copy(u_out, u_ref, store_sem.at[1])
    store_u.start()
    store_q.wait()
    store_u.wait()


def applied(first_factor, first_inverse, gap, cross, panel, trailing):
    rows = panel.shape[0]
    vmem = pl.BlockSpec(memory_space=pltpu.VMEM)
    hbm = pl.BlockSpec(memory_space=pltpu.HBM)
    dma = pltpu.SemaphoreType.DMA
    return pl.pallas_call(
        apply_kernel,
        out_shape=[
            jax.ShapeDtypeStruct((rows, ORDER), f32),
            jax.ShapeDtypeStruct((ORDER, ORDER), f32),
            jax.ShapeDtypeStruct((ORDER, TRAIL), f32),
            jax.ShapeDtypeStruct((rows, TRAIL), f32),
        ],
        in_specs=[vmem] * 4 + [hbm] * 2,
        out_specs=[hbm, vmem, vmem, hbm],
        scratch_shapes=[
            pltpu.VMEM((rows, ORDER), f32),
            pltpu.VMEM((rows, TRAIL), f32),
            pltpu.VMEM((rows, ORDER), f32),
            pltpu.VMEM((rows, TRAIL), f32),
            pltpu.VMEM((ORDER, ORDER), f32),
            dma((2,)),
            dma((2,)),
        ],
        compiler_params=pltpu.CompilerParams(vmem_limit_bytes=62 * 2**20),
        name="apply_factor",
    )(first_factor, first_inverse, gap, cross, panel, trailing)


def solution(mesh):
    nz = mesh.shape["wide"] // (NY * NC)

    def on_device(panel, trailing):
        row_total = float(panel.shape[0] * mesh.size)
        parts = reduced(panel, trailing, nz, row_total)
        q_factor, r_factor, projection, updated = applied(*parts, panel, trailing)
        return q_factor, r_factor, projection, updated

    rows = P(("wide", "narrow"), None)
    return jax.shard_map(
        on_device, mesh=mesh, in_specs=(rows, rows), out_specs=(rows, P(), P(), rows),
        check_vma=False,
    )
```

```python
import functools

import jax
import jax.numpy as jnp
from jax import lax
from jax.experimental import pallas as pl
from jax.experimental.pallas import tpu as pltpu
from jax.sharding import PartitionSpec as P

f32 = jnp.float32
bf16 = jnp.bfloat16
HIGHEST = lax.Precision.HIGHEST
MESH = pl.DeviceIdType.MESH

ORDER = 128
TRAIL = 256
NX, NY, NC = 4, 4, 2
SHARES = NX * NY * NC
TILE = 8
WIDTH = 16
CHUNKS = 2


def contract(left, right, dims, precision=HIGHEST):
    return lax.dot_general(
        left, right, (dims, ((), ())), precision=precision, preferred_element_type=f32
    )


def two_sum(a, b):
    total = a + b
    part = total - a
    return total, (a - (total - part)) + (b - part)


def slices(values):
    top = jnp.max(jnp.abs(values), axis=0, keepdims=True)
    unit = (top + top * (2.0**-23)) - top
    shift = unit * (1.5 * 2.0**40)
    parts = []
    rest = values
    for _ in range(3):
        part = (rest + shift) - shift
        rest = rest - part
        shift = shift * (2.0**-8)
        parts.append(part.astype(bf16))
    parts.append(rest.astype(bf16))
    return parts


def gram_parts(parts):
    first = contract(parts[0], jnp.concatenate(parts, axis=1), ((0,), (0,)), None)
    second = contract(parts[1], jnp.concatenate(parts[1:], axis=1), ((0,), (0,)), None)
    third = contract(parts[2], parts[2], ((0,), (0,)), None)
    n = ORDER
    cross = first[:, n : 2 * n]
    tail = (first[:, 2 * n : 3 * n] + second[:, n : 2 * n]) + (
        first[:, 3 * n :] + second[:, 2 * n :]
    )
    return first[:, :n], cross + cross.T, (tail + tail.T) + (second[:, :n] + third)


def split(values, count=3):
    parts = []
    for _ in range(count - 1):
        part = values.astype(bf16)
        values = values - part.astype(f32)
        parts.append(part)
    return parts + [values.astype(bf16)]


def factor(work):
    order, width = work.shape[0], WIDTH
    rows = lax.broadcasted_iota(jnp.int32, (order, order), 0)
    cols = lax.broadcasted_iota(jnp.int32, (order, order), 1)
    inverse = jnp.where(rows == cols, 1.0, 0.0).astype(f32)
    sub = lax.broadcasted_iota(jnp.int32, (width, order), 0)
    lane = lax.broadcasted_iota(jnp.int32, (width, order), 1)
    row = lax.broadcasted_iota(jnp.int32, (TILE, order), 0)
    uppers, inverses = [], []
    for start in range(0, order, width):
        top, top_inverse = work[:width], inverse[:width]
        column = jnp.stack(
            [
                jnp.broadcast_to(top[:, start + k : start + k + 1], (width, order))
                for k in range(width)
            ]
        )
        done, done_inverse, pivots = [], [], []
        for i in range(width):
            r = i % TILE
            pivot = column[0, r : r + 1, :]
            held = pivot if r == 0 else jnp.where(row == r, pivot, held)
            if i + 1 < width:
                below = jnp.where(row > r, column[0, :TILE], 0.0)
                if column.shape[1] > TILE:
                    below = jnp.concatenate([below, column[0, TILE:]], axis=0)
                ratio = below * (1.0 / pivot)
                column = column[1:] - ratio[None] * column[1:, r : r + 1, :]
                top = top - ratio * top[r : r + 1, :]
                top_inverse = top_inverse - ratio * top_inverse[r : r + 1, :]
            if r == TILE - 1:
                done.append(top[:TILE])
                done_inverse.append(top_inverse[:TILE])
                pivots.append(held)
                if i + 1 < width:
                    top, top_inverse, column = top[TILE:], top_inverse[TILE:], column[:, TILE:]
        scale = lax.rsqrt(jnp.concatenate(pivots, axis=0))
        upper = jnp.concatenate(done, axis=0) * scale
        lower = jnp.concatenate(done_inverse, axis=0) * scale
        uppers.append(jnp.where(sub + start <= lane, upper, 0.0))
        inverses.append(lower)
        if start + width < order:
            a0, a1, a2 = split(upper)
            b0, b1, b2 = split(jnp.concatenate([upper, lower], axis=1))
            left = jnp.concatenate([a0, a0, a1, a0, a2, a1], axis=0).T
            right = jnp.concatenate([b0, b1, b0, b2, b0, b1], axis=0)
            step = contract(left[start + width :], right, ((1,), (0,)), None)
            work = work[width:] - step[:, :order]
            inverse = inverse[width:] - step[:, order:]
    return jnp.concatenate(uppers, axis=0), jnp.concatenate(inverses, axis=0)


def times_square(left, right):
    a0, a1, a2 = left
    b0, b1, b2 = right
    nn = ((1,), (0,))
    pair = jnp.concatenate([jnp.concatenate([b0, b1], axis=1)] * 2, axis=0)
    most = contract(jnp.concatenate([a0, a1], axis=1), pair, nn, None)
    rest = contract(
        jnp.concatenate([a0, a2], axis=1), jnp.concatenate([b2, b0], axis=0), nn, None
    )
    return most[:, :ORDER] + (most[:, ORDER:] + rest)


def times_wide(left, right):
    a0, a1, a2 = left
    b0, b1, b2 = right
    nn = ((1,), (0,))
    pair = jnp.concatenate([b0, b1], axis=0)
    most = contract(jnp.concatenate([a0, a0], axis=1), pair, nn, None)
    more = contract(jnp.concatenate([a1, a1], axis=1), pair, nn, None)
    rest = contract(
        jnp.concatenate([a0, a2], axis=1), jnp.concatenate([b2, b0], axis=0), nn, None
    )
    return most + (more + rest)


def swap(tiles):
    return pltpu.roll(tiles, 4, tiles.ndim - 2)


def halves(left, right):
    left = left.reshape(ORDER // TILE, TILE, ORDER)
    right = swap(right.reshape(ORDER // TILE, TILE, ORDER))
    low = lax.broadcasted_iota(jnp.int32, left.shape, 1) < 4
    return jnp.where(low, left, right), jnp.where(low, right, left)


def unhalve(even, odd):
    low = lax.broadcasted_iota(jnp.int32, even.shape, 1) < 4
    left = jnp.where(low, even, odd)
    right = swap(jnp.where(low, odd, even))
    return left.reshape(ORDER, ORDER), right.reshape(ORDER, ORDER)


def add_pairs(terms, core):
    sub = lax.broadcasted_iota(jnp.int32, (TILE, ORDER), 0)
    mine = (sub // 4) == core
    total, error = terms[0], jnp.zeros((TILE, ORDER), f32)
    for term in terms[1:]:
        total, more = two_sum(total, term)
        error = error + more
    low = error + swap(total + error)
    high = total + low
    return jnp.where(mine, high, swap(low - (high - total)))


def add_plain(terms):
    while len(terms) > 1:
        terms = [a + b for a, b in zip(terms[::2], terms[1::2])] + (
            [terms[-1]] if len(terms) % 2 else []
        )
    return terms[0]


def reduce_kernel(
    nz, row_total,
    panel_ref, trail_ref, factor_ref, inverse_ref, gap_ref, cross_ref,
    panel, trail, send, rs_in, z_out, z_in, gathered,
    load_sem, rs_send, rs_recv, z_send, z_recv, ag_send, ag_recv,
):
    load_panel = pltpu.make_async_copy(panel_ref, panel, load_sem.at[0])
    load_trail = pltpu.make_async_copy(trail_ref, trail, load_sem.at[1])
    load_panel.start()
    load_trail.start()

    wide, x = lax.axis_index("wide"), lax.axis_index("narrow")
    z, y, core = wide // (NY * NC), (wide // NC) % NY, wide % NC
    share = (x * NY + y) * NC + core

    near = []
    for dx in range(NX):
        for dy in range(NY):
            for dc in range(NC):
                if dx or dy or dc:
                    hops = min(dx, NX - dx) + min(dy, NY - dy)
                    near.append((-hops, dx, dy, dc))
    near = sorted(near)

    def neighbour(dx, dy, dc):
        px, py, pc = (x + dx) % NX, (y + dy) % NY, (core + dc) % NC
        return (px * NY + py) * NC + pc, ((z * NY + py) * NC + pc, px)

    around = [neighbour(dx, dy, dc) for _, dx, dy, dc in near]
    steps = sorted(range(1, nz), key=lambda d: -min(d, nz - d))
    along = [((((z + d) % nz) * NY + y) * NC + core, x) for d in steps]

    barrier = pltpu.get_barrier_semaphore()
    for device in along + [device for _, device in around]:
        pl.semaphore_signal(barrier, inc=1, device_id=device, device_id_type=MESH)

    def copy(src, dst, send_sem, recv_sem, device):
        pltpu.make_async_remote_copy(
            src_ref=src, dst_ref=dst, send_sem=send_sem, recv_sem=recv_sem,
            device_id=device, device_id_type=MESH,
        ).start()

    def scatter(k):
        for slot, (target, device) in enumerate(around):
            copy(
                send.at[k, target // NC, target % NC], rs_in.at[k, slot],
                rs_send.at[k], rs_recv.at[k], device,
            )

    def scattered(k):
        pltpu.make_async_copy(rs_in.at[k], rs_in.at[k], rs_recv.at[k]).wait()
        return [send[k, share // NC, share % NC]] + [rs_in[k, n] for n in range(SHARES - 1)]

    def exchange(k, block):
        z_out[k] = block
        for device in along:
            copy(z_out.at[k], z_in.at[k, z], z_send.at[k], z_recv.at[k], device)
        z_in[k, z] = block

    def exchanged(k):
        others = z_in.at[k, pl.ds(0, nz - 1)]
        pltpu.make_async_copy(others, others, z_recv.at[k]).wait()
        return [z_in[k, n] for n in range(nz)]

    def gather(k, block):
        gathered[k, share] = block
        for _, device in around:
            copy(
                gathered.at[k, share], gathered.at[k, share],
                ag_send.at[k], ag_recv.at[k], device,
            )

    def gathered_pair(k):
        others = gathered.at[k, pl.ds(0, SHARES - 1)]
        pltpu.make_async_copy(others, others, ag_recv.at[k]).wait()
        blocks = gathered[k].reshape(SHARES // NC, NC, TILE, ORDER)
        return unhalve(blocks[:, 0], blocks[:, 1])

    def stage(k, left, right):
        even, odd = halves(left, right)
        send[k, :, 0] = even
        send[k, :, 1] = odd

    load_panel.wait()
    scale = 1.0 / row_total
    parts = slices(panel[...])
    lead, second, third = gram_parts(parts)
    high, error = two_sum(lead, second)
    error = error + third
    total = high + error
    error = error - (total - high)
    stage(0, total * scale, error * scale)

    pl.semaphore_wait(barrier, len(along) + len(around))
    scatter(0)

    load_trail.wait()
    values = trail[...]
    t0 = values.astype(bf16)
    values = values - t0.astype(f32)
    t1 = values.astype(bf16)
    t2 = (values - t1.astype(f32)).astype(bf16)
    tn = ((0,), (0,))
    both = contract(parts[0], jnp.concatenate([t0, t1, t2], axis=1), tn, None)
    more = contract(parts[1], jnp.concatenate([t0, t1], axis=1), tn, None)
    last = contract(parts[2], t0, tn, None)
    cross = both[:, :TRAIL] + (
        (both[:, TRAIL : 2 * TRAIL] + more[:, :TRAIL])
        + (both[:, 2 * TRAIL :] + more[:, TRAIL:] + last)
    )
    cross = cross * scale
    stage(1, cross[:, :ORDER], cross[:, ORDER:])
    scatter(1)

    exchange(0, add_pairs(scattered(0), core))
    exchange(1, add_plain(scattered(1)))
    gather(0, add_pairs(exchanged(0), core))
    gather(1, add_plain(exchanged(1)))
    high, low = gathered_pair(0)

    nn, nt = ((1,), (0,)), ((1,), (1,))
    first_factor, first_inverse = factor(high)
    factor_ref[...] = first_factor
    inverse_ref[...] = first_inverse
    lead, second, third = gram_parts(slices(first_factor))
    rest, error = two_sum(high, -lead)
    rest, more = two_sum(rest, -second)
    gap = rest + ((error + more) + (low - third))
    gap_ref[...] = contract(contract(first_inverse, gap, nn), first_inverse, nt)

    left, right = gathered_pair(1)
    cross_ref[:, :ORDER] = left
    cross_ref[:, ORDER:] = right

    for k in range(2):
        pltpu.make_async_copy(rs_in.at[k], rs_in.at[k], rs_send.at[k]).wait()
        others = z_in.at[k, pl.ds(0, nz - 1)]
        pltpu.make_async_copy(others, others, z_send.at[k]).wait()
        others = gathered.at[k, pl.ds(0, SHARES - 1)]
        pltpu.make_async_copy(others, others, ag_send.at[k]).wait()


def reduced(panel, trailing, nz, row_total):
    rows = panel.shape[0]
    block = (TILE, ORDER)
    vmem = pl.BlockSpec(memory_space=pltpu.VMEM)
    dma = pltpu.SemaphoreType.DMA
    return pl.pallas_call(
        functools.partial(reduce_kernel, nz, row_total),
        out_shape=[pltpu.VMEM((ORDER, ORDER), f32)] * 3 + [pltpu.VMEM((ORDER, TRAIL), f32)],
        in_specs=[pl.BlockSpec(memory_space=pltpu.HBM)] * 2,
        out_specs=[vmem] * 4,
        scratch_shapes=[
            pltpu.VMEM((rows, ORDER), f32),
            pltpu.VMEM((rows, TRAIL), f32),
            pltpu.VMEM((2, SHARES // NC, NC) + block, f32),
            pltpu.VMEM((2, SHARES - 1) + block, f32),
            pltpu.VMEM((2,) + block, f32),
            pltpu.VMEM((2, nz) + block, f32),
            pltpu.VMEM((2, SHARES) + block, f32),
        ]
        + [dma((2,))] * 7,
        compiler_params=pltpu.CompilerParams(
            collective_id=0, has_side_effects=True, vmem_limit_bytes=62 * 2**20
        ),
        name="reduce_and_factor",
    )(panel, trailing)


def apply_kernel(
    factor_ref, inverse_ref, gap_ref, cross_ref, panel_ref, trail_ref,
    q_ref, r_ref, p_ref, u_ref,
    q_out, u_out, whole, store_sem,
):
    nn, nt, tn = ((1,), (0,)), ((1,), (1,)), ((0,), (0,))
    gap = gap_ref[...]
    rows = lax.broadcasted_iota(jnp.int32, gap.shape, 0)
    cols = lax.broadcasted_iota(jnp.int32, gap.shape, 1)
    eye = jnp.where(rows == cols, 1.0, 0.0).astype(f32)
    weight = jnp.where(rows < cols, 1.0, 0.5 * eye).astype(f32)
    small = jnp.sum(gap * gap) < 0.01

    @pl.when(small)
    def _():
        first_factor, first_inverse, gap = factor_ref[...], inverse_ref[...], gap_ref[...]
        upper = weight * gap
        close = None
        for step in range(4):
            upper = weight * (gap - contract(upper, upper, tn))
            if step == 1:
                close = upper
        once = first_inverse - contract(close, first_inverse, tn)
        guess = first_inverse - contract(close, once, tn)
        left = contract(guess, first_factor, nt)
        rough = contract(guess, cross_ref[...], nn)
        r_ref[...] = first_factor + contract(upper, first_factor, nn)
        rest = (eye - left) - contract(left, upper, nt)
        turned = guess.T
        whole[...] = turned + contract(turned, rest, nt)
        p_ref[...] = rough + contract(rest, rough, nn)

    @pl.when(jnp.logical_not(small))
    def _():
        second_factor, second_inverse = factor(eye + gap_ref[...])
        r_factor = contract(second_factor, factor_ref[...], nn)
        r_ref[...] = r_factor
        guess = contract(second_inverse, inverse_ref[...], nn)
        inverse = guess + contract(eye - contract(guess, r_factor, nt), guess, nn)
        whole[...] = inverse.T
        p_ref[...] = contract(inverse, cross_ref[...], nn)

    inverse, projection = split(whole[...]), split(p_ref[...])
    size = panel_ref.shape[0] // CHUNKS
    stores = []
    for k in range(CHUNKS):
        part = pl.ds(k * size, size)
        q_factor = times_square(split(panel_ref[part]), inverse)
        q_out[part] = q_factor
        stores.append(pltpu.make_async_copy(q_out.at[part], q_ref.at[part], store_sem.at[0, k]))
        stores[-1].start()
        u_out[part] = trail_ref[part] - times_wide(split(q_factor), projection)
        stores.append(pltpu.make_async_copy(u_out.at[part], u_ref.at[part], store_sem.at[1, k]))
        stores[-1].start()
    for store in stores:
        store.wait()


def applied(first_factor, first_inverse, gap, cross, panel, trailing):
    rows = panel.shape[0]
    vmem = pl.BlockSpec(memory_space=pltpu.VMEM)
    hbm = pl.BlockSpec(memory_space=pltpu.HBM)
    dma = pltpu.SemaphoreType.DMA
    return pl.pallas_call(
        apply_kernel,
        out_shape=[
            jax.ShapeDtypeStruct((rows, ORDER), f32),
            jax.ShapeDtypeStruct((ORDER, ORDER), f32),
            jax.ShapeDtypeStruct((ORDER, TRAIL), f32),
            jax.ShapeDtypeStruct((rows, TRAIL), f32),
        ],
        in_specs=[vmem] * 6,
        out_specs=[hbm, vmem, vmem, hbm],
        scratch_shapes=[
            pltpu.VMEM((rows, ORDER), f32),
            pltpu.VMEM((rows, TRAIL), f32),
            pltpu.VMEM((ORDER, ORDER), f32),
            dma((2, CHUNKS)),
        ],
        compiler_params=pltpu.CompilerParams(vmem_limit_bytes=32 * 2**20),
        name="apply_factor",
    )(first_factor, first_inverse, gap, cross, panel, trailing)


def solution(mesh):
    nz = mesh.shape["wide"] // (NY * NC)

    def on_device(panel, trailing):
        row_total = float(panel.shape[0] * mesh.size)
        parts = reduced(panel, trailing, nz, row_total)
        q_factor, r_factor, projection, updated = applied(*parts, panel, trailing)
        return q_factor, r_factor, projection, updated

    rows = P(("wide", "narrow"), None)
    return jax.shard_map(
        on_device, mesh=mesh, in_specs=(rows, rows), out_specs=(rows, P(), P(), rows),
        check_vma=False,
    )
```

```python
import functools

import jax
import jax.numpy as jnp
from jax import lax
from jax.experimental import pallas as pl
from jax.experimental.pallas import tpu as pltpu
from jax.sharding import PartitionSpec as P

f32 = jnp.float32
bf16 = jnp.bfloat16
HIGHEST = lax.Precision.HIGHEST
MESH = pl.DeviceIdType.MESH

ORDER = 128
TRAIL = 256
NX, NY, NC = 4, 4, 2
SHARES = NX * NY * NC
TILE = 8
WIDTH = 16
CHUNKS = 2
STEPS = 3


def contract(left, right, dims, precision=HIGHEST):
    return lax.dot_general(
        left, right, (dims, ((), ())), precision=precision, preferred_element_type=f32
    )


def two_sum(a, b):
    total = a + b
    part = total - a
    return total, (a - (total - part)) + (b - part)


def slices(values):
    top = jnp.max(jnp.abs(values), axis=0, keepdims=True)
    unit = (top + top * (2.0**-23)) - top
    shift = unit * (1.5 * 2.0**40)
    parts = []
    rest = values
    for _ in range(3):
        part = (rest + shift) - shift
        rest = rest - part
        shift = shift * (2.0**-8)
        parts.append(part.astype(bf16))
    parts.append(rest.astype(bf16))
    return parts


def gram_parts(parts):
    first = contract(parts[0], jnp.concatenate(parts, axis=1), ((0,), (0,)), None)
    second = contract(parts[1], jnp.concatenate(parts[1:], axis=1), ((0,), (0,)), None)
    third = contract(parts[2], parts[2], ((0,), (0,)), None)
    n = ORDER
    cross = first[:, n : 2 * n]
    tail = (first[:, 2 * n : 3 * n] + second[:, n : 2 * n]) + (
        first[:, 3 * n :] + second[:, 2 * n :]
    )
    return first[:, :n], cross + cross.T, (tail + tail.T) + (second[:, :n] + third)


def split(values, count=3):
    parts = []
    for _ in range(count - 1):
        part = values.astype(bf16)
        values = values - part.astype(f32)
        parts.append(part)
    return parts + [values.astype(bf16)]


def factor(work):
    order, width = work.shape[0], WIDTH
    rows = lax.broadcasted_iota(jnp.int32, (order, order), 0)
    cols = lax.broadcasted_iota(jnp.int32, (order, order), 1)
    inverse = jnp.where(rows == cols, 1.0, 0.0).astype(f32)
    sub = lax.broadcasted_iota(jnp.int32, (width, order), 0)
    lane = lax.broadcasted_iota(jnp.int32, (width, order), 1)
    row = lax.broadcasted_iota(jnp.int32, (TILE, order), 0)
    uppers, inverses = [], []
    for start in range(0, order, width):
        top, top_inverse = work[:width], inverse[:width]
        column = jnp.stack(
            [
                jnp.broadcast_to(top[:, start + k : start + k + 1], (width, order))
                for k in range(width)
            ]
        )
        done, done_inverse, pivots = [], [], []
        for i in range(width):
            r = i % TILE
            pivot = column[0, r : r + 1, :]
            held = pivot if r == 0 else jnp.where(row == r, pivot, held)
            if i + 1 < width:
                below = jnp.where(row > r, column[0, :TILE], 0.0)
                if column.shape[1] > TILE:
                    below = jnp.concatenate([below, column[0, TILE:]], axis=0)
                ratio = below * (1.0 / pivot)
                column = column[1:] - ratio[None] * column[1:, r : r + 1, :]
                top = top - ratio * top[r : r + 1, :]
                top_inverse = top_inverse - ratio * top_inverse[r : r + 1, :]
            if r == TILE - 1:
                done.append(top[:TILE])
                done_inverse.append(top_inverse[:TILE])
                pivots.append(held)
                if i + 1 < width:
                    top, top_inverse, column = top[TILE:], top_inverse[TILE:], column[:, TILE:]
        scale = lax.rsqrt(jnp.concatenate(pivots, axis=0))
        upper = jnp.concatenate(done, axis=0) * scale
        lower = jnp.concatenate(done_inverse, axis=0) * scale
        uppers.append(jnp.where(sub + start <= lane, upper, 0.0))
        inverses.append(lower)
        if start + width < order:
            a0, a1, a2 = split(upper)
            b0, b1, b2 = split(jnp.concatenate([upper, lower], axis=1))
            left = jnp.concatenate([a0, a0, a1, a0, a2, a1], axis=0).T
            right = jnp.concatenate([b0, b1, b0, b2, b0, b1], axis=0)
            step = contract(left[start + width :], right, ((1,), (0,)), None)
            work = work[width:] - step[:, :order]
            inverse = inverse[width:] - step[:, order:]
    return jnp.concatenate(uppers, axis=0), jnp.concatenate(inverses, axis=0)


def times_close(left, right, turned=False):
    a0, a1 = split(left, 2)
    b0, b1 = split(right, 2)
    sides = jnp.concatenate([a0, a1], axis=1)
    if turned:
        rows = jnp.concatenate([b0, b1], axis=0)
        both = contract(sides, jnp.concatenate([rows, rows], axis=1), ((1,), (1,)), None)
    else:
        rows = jnp.concatenate([b0, b1], axis=1)
        both = contract(sides, jnp.concatenate([rows, rows], axis=0), ((1,), (0,)), None)
    return both[:, :ORDER] + both[:, ORDER:]


def times_square(left, right):
    a0, a1, a2 = left
    b0, b1, b2 = right
    nn = ((1,), (0,))
    pair = jnp.concatenate([jnp.concatenate([b0, b1], axis=1)] * 2, axis=0)
    most = contract(jnp.concatenate([a0, a1], axis=1), pair, nn, None)
    rest = contract(
        jnp.concatenate([a0, a2], axis=1), jnp.concatenate([b2, b0], axis=0), nn, None
    )
    return most[:, :ORDER] + (most[:, ORDER:] + rest)


def times_wide(left, right):
    a0, a1, a2 = left
    b0, b1, b2 = right
    nn = ((1,), (0,))
    pair = jnp.concatenate([b0, b1], axis=0)
    most = contract(jnp.concatenate([a0, a0], axis=1), pair, nn, None)
    more = contract(jnp.concatenate([a1, a1], axis=1), pair, nn, None)
    rest = contract(
        jnp.concatenate([a0, a2], axis=1), jnp.concatenate([b2, b0], axis=0), nn, None
    )
    return most + (more + rest)


def swap(tiles):
    return pltpu.roll(tiles, 4, tiles.ndim - 2)


def halves(left, right):
    left = left.reshape(ORDER // TILE, TILE, ORDER)
    right = swap(right.reshape(ORDER // TILE, TILE, ORDER))
    low = lax.broadcasted_iota(jnp.int32, left.shape, 1) < 4
    return jnp.where(low, left, right), jnp.where(low, right, left)


def unhalve(even, odd):
    low = lax.broadcasted_iota(jnp.int32, even.shape, 1) < 4
    left = jnp.where(low, even, odd)
    right = swap(jnp.where(low, odd, even))
    return left.reshape(ORDER, ORDER), right.reshape(ORDER, ORDER)


def add_pairs(terms, core):
    sub = lax.broadcasted_iota(jnp.int32, (TILE, ORDER), 0)
    mine = (sub // 4) == core
    total, error = terms[0], jnp.zeros((TILE, ORDER), f32)
    for term in terms[1:]:
        total, more = two_sum(total, term)
        error = error + more
    low = error + swap(total + error)
    high = total + low
    return jnp.where(mine, high, swap(low - (high - total)))


def add_plain(terms):
    while len(terms) > 1:
        terms = [a + b for a, b in zip(terms[::2], terms[1::2])] + (
            [terms[-1]] if len(terms) % 2 else []
        )
    return terms[0]


def reduce_kernel(
    nz, row_total,
    panel_ref, trail_ref, factor_ref, inverse_ref, gap_ref, cross_ref,
    panel, trail, send, rs_in, z_out, z_in, gathered,
    load_sem, rs_send, rs_recv, z_send, z_recv, ag_send, ag_recv,
):
    wide, x = lax.axis_index("wide"), lax.axis_index("narrow")
    z, y, core = wide // (NY * NC), (wide // NC) % NY, wide % NC
    share = (x * NY + y) * NC + core

    near = []
    for dx in range(NX):
        for dy in range(NY):
            for dc in range(NC):
                if dx or dy or dc:
                    hops = min(dx, NX - dx) + min(dy, NY - dy)
                    near.append((-hops, dx, dy, dc))
    near = sorted(near)

    def neighbour(dx, dy, dc):
        px, py, pc = (x + dx) % NX, (y + dy) % NY, (core + dc) % NC
        return (px * NY + py) * NC + pc, ((z * NY + py) * NC + pc, px)

    around = [neighbour(dx, dy, dc) for _, dx, dy, dc in near]
    steps = sorted(range(1, nz), key=lambda d: -min(d, nz - d))
    along = [((((z + d) % nz) * NY + y) * NC + core, x) for d in steps]

    barrier = pltpu.get_barrier_semaphore()
    for device in [device for _, device in around] + along:
        pl.semaphore_signal(barrier, inc=1, device_id=device, device_id_type=MESH)

    load_panel = pltpu.make_async_copy(panel_ref, panel, load_sem.at[0])
    load_trail = pltpu.make_async_copy(trail_ref, trail, load_sem.at[1])
    load_panel.start()
    load_trail.start()

    def copy(src, dst, send_sem, recv_sem, device):
        pltpu.make_async_remote_copy(
            src_ref=src, dst_ref=dst, send_sem=send_sem, recv_sem=recv_sem,
            device_id=device, device_id_type=MESH,
        ).start()

    def scatter(k):
        for slot, (target, device) in enumerate(around):
            copy(
                send.at[k, target // NC, target % NC], rs_in.at[k, slot],
                rs_send.at[k], rs_recv.at[k], device,
            )

    def scattered(k):
        pltpu.make_async_copy(rs_in.at[k], rs_in.at[k], rs_recv.at[k]).wait()
        return [send[k, share // NC, share % NC]] + [rs_in[k, n] for n in range(SHARES - 1)]

    def exchange(k, block):
        z_out[k] = block
        for device in along:
            copy(z_out.at[k], z_in.at[k, z], z_send.at[k], z_recv.at[k], device)
        z_in[k, z] = block

    def exchanged(k):
        others = z_in.at[k, pl.ds(0, nz - 1)]
        pltpu.make_async_copy(others, others, z_recv.at[k]).wait()
        return [z_in[k, n] for n in range(nz)]

    def gather(k, block):
        gathered[k, share] = block
        for _, device in around:
            copy(
                gathered.at[k, share], gathered.at[k, share],
                ag_send.at[k], ag_recv.at[k], device,
            )

    def gathered_pair(k):
        others = gathered.at[k, pl.ds(0, SHARES - 1)]
        pltpu.make_async_copy(others, others, ag_recv.at[k]).wait()
        blocks = gathered[k].reshape(SHARES // NC, NC, TILE, ORDER)
        return unhalve(blocks[:, 0], blocks[:, 1])

    def stage(k, left, right):
        even, odd = halves(left, right)
        send[k, :, 0] = even
        send[k, :, 1] = odd

    load_panel.wait()
    scale = 1.0 / row_total
    parts = slices(panel[...])
    lead, second, third = gram_parts(parts)
    high, error = two_sum(lead, second)
    error = error + third
    total = high + error
    error = error - (total - high)
    stage(0, total * scale, error * scale)

    pl.semaphore_wait(barrier, len(along) + len(around))
    scatter(0)

    load_trail.wait()
    values = trail[...]
    t0 = values.astype(bf16)
    values = values - t0.astype(f32)
    t1 = values.astype(bf16)
    t2 = (values - t1.astype(f32)).astype(bf16)
    tn = ((0,), (0,))
    both = contract(parts[0], jnp.concatenate([t0, t1, t2], axis=1), tn, None)
    more = contract(parts[1], jnp.concatenate([t0, t1], axis=1), tn, None)
    last = contract(parts[2], t0, tn, None)
    cross = both[:, :TRAIL] + (
        (both[:, TRAIL : 2 * TRAIL] + more[:, :TRAIL])
        + (both[:, 2 * TRAIL :] + more[:, TRAIL:] + last)
    )
    cross = cross * scale
    stage(1, cross[:, :ORDER], cross[:, ORDER:])
    scatter(1)

    exchange(0, add_pairs(scattered(0), core))
    exchange(1, add_plain(scattered(1)))
    gather(0, add_pairs(exchanged(0), core))
    gather(1, add_plain(exchanged(1)))
    high, low = gathered_pair(0)

    first_factor, first_inverse = factor(high)
    factor_ref[...] = first_factor
    inverse_ref[...] = first_inverse
    lead, second, third = gram_parts(slices(first_factor))
    rest, error = two_sum(high, -lead)
    rest, more = two_sum(rest, -second)
    gap = rest + ((error + more) + (low - third))
    gap_ref[...] = times_close(times_close(first_inverse, gap), first_inverse, turned=True)

    left, right = gathered_pair(1)
    cross_ref[:, :ORDER] = left
    cross_ref[:, ORDER:] = right

    for k in range(2):
        pltpu.make_async_copy(rs_in.at[k], rs_in.at[k], rs_send.at[k]).wait()
        others = z_in.at[k, pl.ds(0, nz - 1)]
        pltpu.make_async_copy(others, others, z_send.at[k]).wait()
        others = gathered.at[k, pl.ds(0, SHARES - 1)]
        pltpu.make_async_copy(others, others, ag_send.at[k]).wait()


def reduced(panel, trailing, nz, row_total):
    rows = panel.shape[0]
    block = (TILE, ORDER)
    vmem = pl.BlockSpec(memory_space=pltpu.VMEM)
    dma = pltpu.SemaphoreType.DMA
    return pl.pallas_call(
        functools.partial(reduce_kernel, nz, row_total),
        out_shape=[pltpu.VMEM((ORDER, ORDER), f32)] * 3 + [pltpu.VMEM((ORDER, TRAIL), f32)],
        in_specs=[pl.BlockSpec(memory_space=pltpu.HBM)] * 2,
        out_specs=[vmem] * 4,
        scratch_shapes=[
            pltpu.VMEM((rows, ORDER), f32),
            pltpu.VMEM((rows, TRAIL), f32),
            pltpu.VMEM((2, SHARES // NC, NC) + block, f32),
            pltpu.VMEM((2, SHARES - 1) + block, f32),
            pltpu.VMEM((2,) + block, f32),
            pltpu.VMEM((2, nz) + block, f32),
            pltpu.VMEM((2, SHARES) + block, f32),
        ]
        + [dma((2,))] * 7,
        compiler_params=pltpu.CompilerParams(
            collective_id=0, has_side_effects=True, vmem_limit_bytes=62 * 2**20
        ),
        name="reduce_and_factor",
    )(panel, trailing)


def apply_kernel(
    factor_ref, inverse_ref, gap_ref, cross_ref, panel_ref, trail_ref,
    q_ref, r_ref, p_ref, u_ref,
    q_out, r_out, p_out, u_out, whole, small_sem, store_sem,
):
    nn, nt = ((1,), (0,)), ((1,), (1,))
    gap, first_factor, first_inverse = gap_ref[...], factor_ref[...], inverse_ref[...]
    rows = lax.broadcasted_iota(jnp.int32, gap.shape, 0)
    cols = lax.broadcasted_iota(jnp.int32, gap.shape, 1)
    eye = jnp.where(rows == cols, 1.0, 0.0).astype(f32)
    weight = jnp.where(rows > cols, 1.0, 0.5 * eye).astype(f32)
    small = jnp.sum(gap * gap) < 0.005

    start = contract(first_inverse, first_factor, nt)
    lower = weight * gap
    close = None
    for step in range(STEPS):
        lower = weight * (gap - times_close(lower, lower, turned=True))
        if step == 0:
            close = lower
    guess = first_inverse - times_close(close, first_inverse)
    guess = first_inverse - times_close(close, guess)
    left = start - times_close(close, start)
    left = start - times_close(close, left)
    rough = contract(guess, cross_ref[...], nn)
    turned = guess.T
    rest = (eye - left) - times_close(left, lower)
    whole[...] = turned + times_close(turned, rest, turned=True)
    p_out[...] = rough + contract(rest, rough, nn)
    r_out[...] = first_factor + times_close(lower.T, first_factor)

    @pl.when(jnp.logical_not(small))
    def _():
        second_factor, second_inverse = factor(eye + gap_ref[...])
        r_factor = contract(second_factor, factor_ref[...], nn)
        r_out[...] = r_factor
        guess = contract(second_inverse, inverse_ref[...], nn)
        inverse = guess + contract(eye - contract(guess, r_factor, nt), guess, nn)
        whole[...] = inverse.T
        p_out[...] = contract(inverse, cross_ref[...], nn)

    inverse, projection = split(whole[...]), split(p_out[...])
    size = panel_ref.shape[0] // CHUNKS
    stores = [
        pltpu.make_async_copy(r_out, r_ref, small_sem.at[0]),
        pltpu.make_async_copy(p_out, p_ref, small_sem.at[1]),
    ]
    stores[0].start()
    stores[1].start()
    for k in range(CHUNKS):
        part = pl.ds(k * size, size)
        q_factor = times_square(split(panel_ref[part]), inverse)
        q_out[part] = q_factor
        stores.append(pltpu.make_async_copy(q_out.at[part], q_ref.at[part], store_sem.at[0, k]))
        stores[-1].start()
        u_out[part] = trail_ref[part] - times_wide(split(q_factor), projection)
        stores.append(pltpu.make_async_copy(u_out.at[part], u_ref.at[part], store_sem.at[1, k]))
        stores[-1].start()
    for store in stores:
        store.wait()


def applied(first_factor, first_inverse, gap, cross, panel, trailing):
    rows = panel.shape[0]
    vmem = pl.BlockSpec(memory_space=pltpu.VMEM)
    hbm = pl.BlockSpec(memory_space=pltpu.HBM)
    dma = pltpu.SemaphoreType.DMA
    return pl.pallas_call(
        apply_kernel,
        out_shape=[
            jax.ShapeDtypeStruct((rows, ORDER), f32),
            jax.ShapeDtypeStruct((ORDER, ORDER), f32),
            jax.ShapeDtypeStruct((ORDER, TRAIL), f32),
            jax.ShapeDtypeStruct((rows, TRAIL), f32),
        ],
        in_specs=[vmem] * 6,
        out_specs=[hbm] * 4,
        scratch_shapes=[
            pltpu.VMEM((rows, ORDER), f32),
            pltpu.VMEM((ORDER, ORDER), f32),
            pltpu.VMEM((ORDER, TRAIL), f32),
            pltpu.VMEM((rows, TRAIL), f32),
            pltpu.VMEM((ORDER, ORDER), f32),
            dma((2,)),
            dma((2, CHUNKS)),
        ],
        compiler_params=pltpu.CompilerParams(vmem_limit_bytes=32 * 2**20),
        name="apply_factor",
    )(first_factor, first_inverse, gap, cross, panel, trailing)


def solution(mesh):
    nz = mesh.shape["wide"] // (NY * NC)

    def on_device(panel, trailing):
        row_total = float(panel.shape[0] * mesh.size)
        parts = reduced(panel, trailing, nz, row_total)
        q_factor, r_factor, projection, updated = applied(*parts, panel, trailing)
        return q_factor, r_factor, projection, updated

    rows = P(("wide", "narrow"), None)
    return jax.shard_map(
        on_device, mesh=mesh, in_specs=(rows, rows), out_specs=(rows, P(), P(), rows),
        check_vma=False,
    )
```

```python
import functools

import jax
import jax.numpy as jnp
from jax import lax
from jax.experimental import pallas as pl
from jax.experimental.pallas import tpu as pltpu
from jax.sharding import PartitionSpec as P

f32 = jnp.float32
bf16 = jnp.bfloat16
HIGHEST = lax.Precision.HIGHEST
MESH = pl.DeviceIdType.MESH

ORDER = 128
TRAIL = 256
NX, NY, NC = 4, 4, 2
SHARES = NX * NY * NC
TILE = 8
WIDTH = 16
CHUNKS = 2
STEPS = 3


def contract(left, right, dims, precision=HIGHEST):
    return lax.dot_general(
        left, right, (dims, ((), ())), precision=precision, preferred_element_type=f32
    )


def two_sum(a, b):
    total = a + b
    part = total - a
    return total, (a - (total - part)) + (b - part)


def slices(values):
    top = jnp.max(jnp.abs(values), axis=0, keepdims=True)
    unit = (top + top * (2.0**-23)) - top
    shift = unit * (1.5 * 2.0**40)
    parts = []
    rest = values
    for _ in range(3):
        part = (rest + shift) - shift
        rest = rest - part
        shift = shift * (2.0**-8)
        parts.append(part.astype(bf16))
    parts.append(rest.astype(bf16))
    return parts


def gram_parts(parts):
    first = contract(parts[0], jnp.concatenate(parts, axis=1), ((0,), (0,)), None)
    second = contract(parts[1], jnp.concatenate(parts[1:], axis=1), ((0,), (0,)), None)
    third = contract(parts[2], parts[2], ((0,), (0,)), None)
    n = ORDER
    cross = first[:, n : 2 * n]
    tail = (first[:, 2 * n : 3 * n] + second[:, n : 2 * n]) + (
        first[:, 3 * n :] + second[:, 2 * n :]
    )
    return first[:, :n], cross + cross.T, (tail + tail.T) + (second[:, :n] + third)


def split(values, count=3):
    parts = []
    for _ in range(count - 1):
        part = values.astype(bf16)
        values = values - part.astype(f32)
        parts.append(part)
    return parts + [values.astype(bf16)]


def factor(work):
    order, width = work.shape[0], WIDTH
    rows = lax.broadcasted_iota(jnp.int32, (order, order), 0)
    cols = lax.broadcasted_iota(jnp.int32, (order, order), 1)
    inverse = jnp.where(rows == cols, 1.0, 0.0).astype(f32)
    sub = lax.broadcasted_iota(jnp.int32, (width, order), 0)
    lane = lax.broadcasted_iota(jnp.int32, (width, order), 1)
    row = lax.broadcasted_iota(jnp.int32, (TILE, order), 0)
    uppers, inverses = [], []
    for start in range(0, order, width):
        count = min(2 * width, order - start)
        top, top_inverse = work[:count], inverse[:count]
        column = jnp.stack(
            [
                jnp.broadcast_to(top[:, start + k : start + k + 1], (count, order))
                for k in range(width)
            ]
        )
        done, done_inverse, pivots = [], [], []
        for i in range(width):
            r = i % TILE
            pivot = column[0, r : r + 1, :]
            held = pivot if r == 0 else jnp.where(row == r, pivot, held)
            below = jnp.where(row > r, column[0, :TILE], 0.0)
            if column.shape[1] > TILE:
                below = jnp.concatenate([below, column[0, TILE:]], axis=0)
            ratio = below * (1.0 / pivot)
            if i + 1 < width:
                column = column[1:] - ratio[None] * column[1:, r : r + 1, :]
            top = top - ratio * top[r : r + 1, :]
            top_inverse = top_inverse - ratio * top_inverse[r : r + 1, :]
            if r == TILE - 1:
                done.append(top[:TILE])
                done_inverse.append(top_inverse[:TILE])
                pivots.append(held)
                if top.shape[0] > TILE:
                    top, top_inverse = top[TILE:], top_inverse[TILE:]
                if i + 1 < width:
                    column = column[:, TILE:]
        scale = lax.rsqrt(jnp.concatenate(pivots, axis=0))
        upper = jnp.concatenate(done, axis=0) * scale
        lower = jnp.concatenate(done_inverse, axis=0) * scale
        uppers.append(jnp.where(sub + start <= lane, upper, 0.0))
        inverses.append(lower)
        if start + count < order:
            a0, a1, a2 = split(upper)
            b0, b1, b2 = split(jnp.concatenate([upper, lower], axis=1))
            left = jnp.concatenate([a0, a0, a1, a0, a2, a1], axis=0).T
            right = jnp.concatenate([b0, b1, b0, b2, b0, b1], axis=0)
            step = contract(left[start + count :], right, ((1,), (0,)), None)
            work = jnp.concatenate([top, work[count:] - step[:, :order]], axis=0)
            inverse = jnp.concatenate([top_inverse, inverse[count:] - step[:, order:]], axis=0)
        else:
            work, inverse = top, top_inverse
    return jnp.concatenate(uppers, axis=0), jnp.concatenate(inverses, axis=0)


def times_close(left, right, turned=False):
    a0, a1 = split(left, 2)
    b0, b1 = split(right, 2)
    sides = jnp.concatenate([a0, a1], axis=1)
    if turned:
        rows = jnp.concatenate([b0, b1], axis=0)
        both = contract(sides, jnp.concatenate([rows, rows], axis=1), ((1,), (1,)), None)
    else:
        rows = jnp.concatenate([b0, b1], axis=1)
        both = contract(sides, jnp.concatenate([rows, rows], axis=0), ((1,), (0,)), None)
    return both[:, :ORDER] + both[:, ORDER:]


def times_square(left, right):
    a0, a1, a2 = left
    b0, b1, b2 = right
    nn = ((1,), (0,))
    pair = jnp.concatenate([jnp.concatenate([b0, b1], axis=1)] * 2, axis=0)
    most = contract(jnp.concatenate([a0, a1], axis=1), pair, nn, None)
    rest = contract(
        jnp.concatenate([a0, a2], axis=1), jnp.concatenate([b2, b0], axis=0), nn, None
    )
    return most[:, :ORDER] + (most[:, ORDER:] + rest)


def times_wide(left, right):
    a0, a1, a2 = left
    b0, b1, b2 = right
    nn = ((1,), (0,))
    pair = jnp.concatenate([b0, b1], axis=0)
    most = contract(jnp.concatenate([a0, a0], axis=1), pair, nn, None)
    more = contract(jnp.concatenate([a1, a1], axis=1), pair, nn, None)
    rest = contract(
        jnp.concatenate([a0, a2], axis=1), jnp.concatenate([b2, b0], axis=0), nn, None
    )
    return most + (more + rest)


def swap(tiles):
    return pltpu.roll(tiles, 4, tiles.ndim - 2)


def halves(left, right):
    left = left.reshape(ORDER // TILE, TILE, ORDER)
    right = swap(right.reshape(ORDER // TILE, TILE, ORDER))
    low = lax.broadcasted_iota(jnp.int32, left.shape, 1) < 4
    return jnp.where(low, left, right), jnp.where(low, right, left)


def unhalve(even, odd):
    low = lax.broadcasted_iota(jnp.int32, even.shape, 1) < 4
    left = jnp.where(low, even, odd)
    right = swap(jnp.where(low, odd, even))
    return left.reshape(ORDER, ORDER), right.reshape(ORDER, ORDER)


def add_pairs(terms, core):
    sub = lax.broadcasted_iota(jnp.int32, (TILE, ORDER), 0)
    mine = (sub // 4) == core
    total, error = terms[0], jnp.zeros((TILE, ORDER), f32)
    for term in terms[1:]:
        total, more = two_sum(total, term)
        error = error + more
    low = error + swap(total + error)
    high = total + low
    return jnp.where(mine, high, swap(low - (high - total)))


def add_plain(terms):
    while len(terms) > 1:
        terms = [a + b for a, b in zip(terms[::2], terms[1::2])] + (
            [terms[-1]] if len(terms) % 2 else []
        )
    return terms[0]


def reduce_kernel(
    nz, row_total,
    panel_ref, trail_ref, factor_ref, inverse_ref, gap_ref, cross_ref,
    panel, trail, send, rs_in, z_out, z_in, gathered,
    load_sem, rs_send, rs_recv, z_send, z_recv, ag_send, ag_recv,
):
    wide, x = lax.axis_index("wide"), lax.axis_index("narrow")
    z, y, core = wide // (NY * NC), (wide // NC) % NY, wide % NC
    share = (x * NY + y) * NC + core

    near = []
    for dx in range(NX):
        for dy in range(NY):
            for dc in range(NC):
                if dx or dy or dc:
                    hops = min(dx, NX - dx) + min(dy, NY - dy)
                    near.append((-hops, dx, dy, dc))
    near = sorted(near)

    def neighbour(dx, dy, dc):
        px, py, pc = (x + dx) % NX, (y + dy) % NY, (core + dc) % NC
        return (px * NY + py) * NC + pc, ((z * NY + py) * NC + pc, px)

    around = [neighbour(dx, dy, dc) for _, dx, dy, dc in near]
    steps = sorted(range(1, nz), key=lambda d: -min(d, nz - d))
    along = [((((z + d) % nz) * NY + y) * NC + core, x) for d in steps]

    barrier = pltpu.get_barrier_semaphore()
    for device in [device for _, device in around] + along:
        pl.semaphore_signal(barrier, inc=1, device_id=device, device_id_type=MESH)

    load_panel = pltpu.make_async_copy(panel_ref, panel, load_sem.at[0])
    load_trail = pltpu.make_async_copy(trail_ref, trail, load_sem.at[1])
    load_panel.start()
    load_trail.start()

    def copy(src, dst, send_sem, recv_sem, device):
        pltpu.make_async_remote_copy(
            src_ref=src, dst_ref=dst, send_sem=send_sem, recv_sem=recv_sem,
            device_id=device, device_id_type=MESH,
        ).start()

    def scatter(k):
        for slot, (target, device) in enumerate(around):
            copy(
                send.at[k, target // NC, target % NC], rs_in.at[k, slot],
                rs_send.at[k], rs_recv.at[k], device,
            )

    def scattered(k):
        pltpu.make_async_copy(rs_in.at[k], rs_in.at[k], rs_recv.at[k]).wait()
        return [send[k, share // NC, share % NC]] + [rs_in[k, n] for n in range(SHARES - 1)]

    def exchange(k, block):
        z_out[k] = block
        for device in along:
            copy(z_out.at[k], z_in.at[k, z], z_send.at[k], z_recv.at[k], device)
        z_in[k, z] = block

    def exchanged(k):
        others = z_in.at[k, pl.ds(0, nz - 1)]
        pltpu.make_async_copy(others, others, z_recv.at[k]).wait()
        return [z_in[k, n] for n in range(nz)]

    def gather(k, block):
        gathered[k, share] = block
        for _, device in around:
            copy(
                gathered.at[k, share], gathered.at[k, share],
                ag_send.at[k], ag_recv.at[k], device,
            )

    def gathered_pair(k):
        others = gathered.at[k, pl.ds(0, SHARES - 1)]
        pltpu.make_async_copy(others, others, ag_recv.at[k]).wait()
        blocks = gathered[k].reshape(SHARES // NC, NC, TILE, ORDER)
        return unhalve(blocks[:, 0], blocks[:, 1])

    def stage(k, left, right):
        even, odd = halves(left, right)
        send[k, :, 0] = even
        send[k, :, 1] = odd

    load_panel.wait()
    scale = 1.0 / row_total
    parts = slices(panel[...])
    lead, second, third = gram_parts(parts)
    high, error = two_sum(lead, second)
    error = error + third
    total = high + error
    error = error - (total - high)
    stage(0, total * scale, error * scale)

    pl.semaphore_wait(barrier, len(along) + len(around))
    scatter(0)

    load_trail.wait()
    values = trail[...]
    t0 = values.astype(bf16)
    values = values - t0.astype(f32)
    t1 = values.astype(bf16)
    t2 = (values - t1.astype(f32)).astype(bf16)
    tn = ((0,), (0,))
    both = contract(parts[0], jnp.concatenate([t0, t1, t2], axis=1), tn, None)
    more = contract(parts[1], jnp.concatenate([t0, t1], axis=1), tn, None)
    last = contract(parts[2], t0, tn, None)
    cross = both[:, :TRAIL] + (
        (both[:, TRAIL : 2 * TRAIL] + more[:, :TRAIL])
        + (both[:, 2 * TRAIL :] + more[:, TRAIL:] + last)
    )
    cross = cross * scale
    stage(1, cross[:, :ORDER], cross[:, ORDER:])
    scatter(1)

    exchange(0, add_pairs(scattered(0), core))
    exchange(1, add_plain(scattered(1)))
    gather(0, add_pairs(exchanged(0), core))
    gather(1, add_plain(exchanged(1)))
    high, low = gathered_pair(0)

    first_factor, first_inverse = factor(high)
    factor_ref[...] = first_factor
    inverse_ref[...] = first_inverse
    lead, second, third = gram_parts(slices(first_factor))
    rest, error = two_sum(high, -lead)
    rest, more = two_sum(rest, -second)
    gap = rest + ((error + more) + (low - third))
    gap_ref[...] = times_close(times_close(first_inverse, gap), first_inverse, turned=True)

    left, right = gathered_pair(1)
    cross_ref[:, :ORDER] = left
    cross_ref[:, ORDER:] = right

    for k in range(2):
        pltpu.make_async_copy(rs_in.at[k], rs_in.at[k], rs_send.at[k]).wait()
        others = z_in.at[k, pl.ds(0, nz - 1)]
        pltpu.make_async_copy(others, others, z_send.at[k]).wait()
        others = gathered.at[k, pl.ds(0, SHARES - 1)]
        pltpu.make_async_copy(others, others, ag_send.at[k]).wait()


def reduced(panel, trailing, nz, row_total):
    rows = panel.shape[0]
    block = (TILE, ORDER)
    vmem = pl.BlockSpec(memory_space=pltpu.VMEM)
    dma = pltpu.SemaphoreType.DMA
    return pl.pallas_call(
        functools.partial(reduce_kernel, nz, row_total),
        out_shape=[pltpu.VMEM((ORDER, ORDER), f32)] * 3 + [pltpu.VMEM((ORDER, TRAIL), f32)],
        in_specs=[pl.BlockSpec(memory_space=pltpu.HBM)] * 2,
        out_specs=[vmem] * 4,
        scratch_shapes=[
            pltpu.VMEM((rows, ORDER), f32),
            pltpu.VMEM((rows, TRAIL), f32),
            pltpu.VMEM((2, SHARES // NC, NC) + block, f32),
            pltpu.VMEM((2, SHARES - 1) + block, f32),
            pltpu.VMEM((2,) + block, f32),
            pltpu.VMEM((2, nz) + block, f32),
            pltpu.VMEM((2, SHARES) + block, f32),
        ]
        + [dma((2,))] * 7,
        compiler_params=pltpu.CompilerParams(
            collective_id=0, has_side_effects=True, vmem_limit_bytes=62 * 2**20
        ),
        name="reduce_and_factor",
    )(panel, trailing)


def apply_kernel(
    factor_ref, inverse_ref, gap_ref, cross_ref, panel_ref, trail_ref,
    q_ref, r_ref, p_ref, u_ref,
    q_out, r_out, p_out, u_out, whole, small_sem, store_sem,
):
    nn, nt = ((1,), (0,)), ((1,), (1,))
    gap, first_factor, first_inverse = gap_ref[...], factor_ref[...], inverse_ref[...]
    rows = lax.broadcasted_iota(jnp.int32, gap.shape, 0)
    cols = lax.broadcasted_iota(jnp.int32, gap.shape, 1)
    eye = jnp.where(rows == cols, 1.0, 0.0).astype(f32)
    weight = jnp.where(rows > cols, 1.0, 0.5 * eye).astype(f32)
    small = jnp.sum(gap * gap) < 0.005

    start = contract(first_inverse, first_factor, nt)
    lower = weight * gap
    close = None
    for step in range(STEPS):
        lower = weight * (gap - times_close(lower, lower, turned=True))
        if step == 0:
            close = lower
    guess = first_inverse - times_close(close, first_inverse)
    guess = first_inverse - times_close(close, guess)
    left = start - times_close(close, start)
    left = start - times_close(close, left)
    rough = contract(guess, cross_ref[...], nn)
    turned = guess.T
    rest = (eye - left) - times_close(left, lower)
    whole[...] = turned + times_close(turned, rest, turned=True)
    p_out[...] = rough + contract(rest, rough, nn)
    r_out[...] = first_factor + times_close(lower.T, first_factor)

    @pl.when(jnp.logical_not(small))
    def _():
        second_factor, second_inverse = factor(eye + gap_ref[...])
        r_factor = contract(second_factor, factor_ref[...], nn)
        r_out[...] = r_factor
        guess = contract(second_inverse, inverse_ref[...], nn)
        inverse = guess + contract(eye - contract(guess, r_factor, nt), guess, nn)
        whole[...] = inverse.T
        p_out[...] = contract(inverse, cross_ref[...], nn)

    inverse, projection = split(whole[...]), split(p_out[...])
    size = panel_ref.shape[0] // CHUNKS
    stores = [
        pltpu.make_async_copy(r_out, r_ref, small_sem.at[0]),
        pltpu.make_async_copy(p_out, p_ref, small_sem.at[1]),
    ]
    stores[0].start()
    stores[1].start()
    for k in range(CHUNKS):
        part = pl.ds(k * size, size)
        q_factor = times_square(split(panel_ref[part]), inverse)
        q_out[part] = q_factor
        stores.append(pltpu.make_async_copy(q_out.at[part], q_ref.at[part], store_sem.at[0, k]))
        stores[-1].start()
        u_out[part] = trail_ref[part] - times_wide(split(q_factor), projection)
        stores.append(pltpu.make_async_copy(u_out.at[part], u_ref.at[part], store_sem.at[1, k]))
        stores[-1].start()
    for store in stores:
        store.wait()


def applied(first_factor, first_inverse, gap, cross, panel, trailing):
    rows = panel.shape[0]
    vmem = pl.BlockSpec(memory_space=pltpu.VMEM)
    hbm = pl.BlockSpec(memory_space=pltpu.HBM)
    dma = pltpu.SemaphoreType.DMA
    return pl.pallas_call(
        apply_kernel,
        out_shape=[
            jax.ShapeDtypeStruct((rows, ORDER), f32),
            jax.ShapeDtypeStruct((ORDER, ORDER), f32),
            jax.ShapeDtypeStruct((ORDER, TRAIL), f32),
            jax.ShapeDtypeStruct((rows, TRAIL), f32),
        ],
        in_specs=[vmem] * 6,
        out_specs=[hbm] * 4,
        scratch_shapes=[
            pltpu.VMEM((rows, ORDER), f32),
            pltpu.VMEM((ORDER, ORDER), f32),
            pltpu.VMEM((ORDER, TRAIL), f32),
            pltpu.VMEM((rows, TRAIL), f32),
            pltpu.VMEM((ORDER, ORDER), f32),
            dma((2,)),
            dma((2, CHUNKS)),
        ],
        compiler_params=pltpu.CompilerParams(vmem_limit_bytes=32 * 2**20),
        name="apply_factor",
    )(first_factor, first_inverse, gap, cross, panel, trailing)


def solution(mesh):
    nz = mesh.shape["wide"] // (NY * NC)

    def on_device(panel, trailing):
        row_total = float(panel.shape[0] * mesh.size)
        parts = reduced(panel, trailing, nz, row_total)
        q_factor, r_factor, projection, updated = applied(*parts, panel, trailing)
        return q_factor, r_factor, projection, updated

    rows = P(("wide", "narrow"), None)
    return jax.shard_map(
        on_device, mesh=mesh, in_specs=(rows, rows), out_specs=(rows, P(), P(), rows),
        check_vma=False,
    )
```

```python
import functools

import jax
import jax.numpy as jnp
from jax import lax
from jax.experimental import pallas as pl
from jax.experimental.pallas import tpu as pltpu
from jax.sharding import PartitionSpec as P

f32 = jnp.float32
bf16 = jnp.bfloat16
HIGHEST = lax.Precision.HIGHEST
MESH = pl.DeviceIdType.MESH

ORDER = 128
TRAIL = 256
NX, NY, NC = 4, 4, 2
SHARES = NX * NY * NC
TILE = 8
WIDTH = 16
CHUNKS = 2
STEPS = 3


def contract(left, right, dims, precision=HIGHEST):
    return lax.dot_general(
        left, right, (dims, ((), ())), precision=precision, preferred_element_type=f32
    )


def two_sum(a, b):
    total = a + b
    part = total - a
    return total, (a - (total - part)) + (b - part)


def slices(values):
    top = jnp.max(jnp.abs(values), axis=0, keepdims=True)
    unit = (top + top * (2.0**-23)) - top
    shift = unit * (1.5 * 2.0**40)
    parts = []
    rest = values
    for _ in range(3):
        part = (rest + shift) - shift
        rest = rest - part
        shift = shift * (2.0**-8)
        parts.append(part.astype(bf16))
    parts.append(rest.astype(bf16))
    return parts


def gram_parts(parts):
    first = contract(parts[0], jnp.concatenate(parts, axis=1), ((0,), (0,)), None)
    second = contract(parts[1], jnp.concatenate(parts[1:], axis=1), ((0,), (0,)), None)
    third = contract(parts[2], parts[2], ((0,), (0,)), None)
    n = ORDER
    cross = first[:, n : 2 * n]
    tail = (first[:, 2 * n : 3 * n] + second[:, n : 2 * n]) + (
        first[:, 3 * n :] + second[:, 2 * n :]
    )
    return first[:, :n], cross + cross.T, (tail + tail.T) + (second[:, :n] + third)


def split(values, count=3):
    parts = []
    for _ in range(count - 1):
        part = values.astype(bf16)
        values = values - part.astype(f32)
        parts.append(part)
    return parts + [values.astype(bf16)]


def factor(work):
    order, width = work.shape[0], WIDTH
    rows = lax.broadcasted_iota(jnp.int32, (order, order), 0)
    cols = lax.broadcasted_iota(jnp.int32, (order, order), 1)
    inverse = jnp.where(rows == cols, 1.0, 0.0).astype(f32)
    sub = lax.broadcasted_iota(jnp.int32, (width, order), 0)
    lane = lax.broadcasted_iota(jnp.int32, (width, order), 1)
    row = lax.broadcasted_iota(jnp.int32, (TILE, order), 0)
    uppers, inverses = [], []
    for start in range(0, order, width):
        count = min(2 * width, order - start)
        top, top_inverse = work[:count], inverse[:count]
        column = jnp.stack(
            [
                jnp.broadcast_to(top[:, start + k : start + k + 1], (count, order))
                for k in range(width)
            ]
        )
        done, done_inverse, pivots = [], [], []
        for i in range(width):
            r = i % TILE
            pivot = column[0, r : r + 1, :]
            held = pivot if r == 0 else jnp.where(row == r, pivot, held)
            below = jnp.where(row > r, column[0, :TILE], 0.0)
            if column.shape[1] > TILE:
                below = jnp.concatenate([below, column[0, TILE:]], axis=0)
            ratio = below * (1.0 / pivot)
            if i + 1 < width:
                column = column[1:] - ratio[None] * column[1:, r : r + 1, :]
            top = top - ratio * top[r : r + 1, :]
            top_inverse = top_inverse - ratio * top_inverse[r : r + 1, :]
            if r == TILE - 1:
                done.append(top[:TILE])
                done_inverse.append(top_inverse[:TILE])
                pivots.append(held)
                if top.shape[0] > TILE:
                    top, top_inverse = top[TILE:], top_inverse[TILE:]
                if i + 1 < width:
                    column = column[:, TILE:]
        scale = lax.rsqrt(jnp.concatenate(pivots, axis=0))
        upper = jnp.concatenate(done, axis=0) * scale
        lower = jnp.concatenate(done_inverse, axis=0) * scale
        uppers.append(jnp.where(sub + start <= lane, upper, 0.0))
        inverses.append(lower)
        if start + count < order:
            a0, a1, a2 = split(upper)
            b0, b1, b2 = split(jnp.concatenate([upper, lower], axis=1))
            left = jnp.concatenate([a0, a0, a1, a0, a2, a1], axis=0).T
            right = jnp.concatenate([b0, b1, b0, b2, b0, b1], axis=0)
            step = contract(left[start + count :], right, ((1,), (0,)), None)
            work = jnp.concatenate([top, work[count:] - step[:, :order]], axis=0)
            inverse = jnp.concatenate([top_inverse, inverse[count:] - step[:, order:]], axis=0)
        else:
            work, inverse = top, top_inverse
    return jnp.concatenate(uppers, axis=0), jnp.concatenate(inverses, axis=0)


def times_close(left, right, turned=False):
    a0, a1 = split(left, 2)
    b0, b1 = split(right, 2)
    sides = jnp.concatenate([a0, a1], axis=1)
    if turned:
        rows = jnp.concatenate([b0, b1], axis=0)
        both = contract(sides, jnp.concatenate([rows, rows], axis=1), ((1,), (1,)), None)
    else:
        rows = jnp.concatenate([b0, b1], axis=1)
        both = contract(sides, jnp.concatenate([rows, rows], axis=0), ((1,), (0,)), None)
    return both[:, :ORDER] + both[:, ORDER:]


def times_square(left, right):
    a0, a1, a2 = left
    b0, b1, b2 = right
    nn = ((1,), (0,))
    pair = jnp.concatenate([jnp.concatenate([b0, b1], axis=1)] * 2, axis=0)
    most = contract(jnp.concatenate([a0, a1], axis=1), pair, nn, None)
    rest = contract(
        jnp.concatenate([a0, a2], axis=1), jnp.concatenate([b2, b0], axis=0), nn, None
    )
    return most[:, :ORDER] + (most[:, ORDER:] + rest)


def times_wide(left, right):
    a0, a1, a2 = left
    b0, b1, b2 = right
    nn = ((1,), (0,))
    pair = jnp.concatenate([b0, b1], axis=0)
    most = contract(jnp.concatenate([a0, a0], axis=1), pair, nn, None)
    more = contract(jnp.concatenate([a1, a1], axis=1), pair, nn, None)
    rest = contract(
        jnp.concatenate([a0, a2], axis=1), jnp.concatenate([b2, b0], axis=0), nn, None
    )
    return most + (more + rest)


def swap(tiles):
    return pltpu.roll(tiles, 4, tiles.ndim - 2)


def halves(left, right):
    left = left.reshape(ORDER // TILE, TILE, ORDER)
    right = swap(right.reshape(ORDER // TILE, TILE, ORDER))
    low = lax.broadcasted_iota(jnp.int32, left.shape, 1) < 4
    return jnp.where(low, left, right), jnp.where(low, right, left)


def unhalve(even, odd):
    low = lax.broadcasted_iota(jnp.int32, even.shape, 1) < 4
    left = jnp.where(low, even, odd)
    right = swap(jnp.where(low, odd, even))
    return left.reshape(ORDER, ORDER), right.reshape(ORDER, ORDER)


def add_pairs(terms, core):
    sub = lax.broadcasted_iota(jnp.int32, (TILE, ORDER), 0)
    mine = (sub // 4) == core
    total, error = terms[0], jnp.zeros((TILE, ORDER), f32)
    for term in terms[1:]:
        total, more = two_sum(total, term)
        error = error + more
    low = error + swap(total + error)
    high = total + low
    return jnp.where(mine, high, swap(low - (high - total)))


def add_plain(terms):
    while len(terms) > 1:
        terms = [a + b for a, b in zip(terms[::2], terms[1::2])] + (
            [terms[-1]] if len(terms) % 2 else []
        )
    return terms[0]


def reduce_kernel(
    nz, row_total,
    panel_ref, trail_ref, factor_ref, inverse_ref, gap_ref, cross_ref,
    panel, trail, send, rs_in, z_out, z_in, gathered,
    load_sem, rs_send, rs_recv, z_send, z_recv, ag_send, ag_recv,
):
    wide, x = lax.axis_index("wide"), lax.axis_index("narrow")
    z, y, core = lax.div(wide, NY * NC), lax.rem(lax.div(wide, NC), NY), lax.rem(wide, NC)
    share = (x * NY + y) * NC + core

    near = []
    for dx in range(NX):
        for dy in range(NY):
            for dc in range(NC):
                if dx or dy or dc:
                    hops = min(dx, NX - dx) + min(dy, NY - dy)
                    near.append((-hops, dx, dy, dc))
    near = sorted(near)

    def neighbour(dx, dy, dc):
        px, py, pc = lax.rem(x + dx, NX), lax.rem(y + dy, NY), lax.rem(core + dc, NC)
        return (px * NY + py) * NC + pc, ((z * NY + py) * NC + pc, px)

    around = [neighbour(dx, dy, dc) for _, dx, dy, dc in near]
    steps = sorted(range(1, nz), key=lambda d: -min(d, nz - d))
    along = [((lax.rem(z + d, nz) * NY + y) * NC + core, x) for d in steps]

    barrier = pltpu.get_barrier_semaphore()
    greeted = [(hops[0], device) for hops, (_, device) in zip(near, around)]
    greeted += [(-min(d, nz - d), device) for d, device in zip(steps, along)]
    for _, device in sorted(greeted, key=lambda entry: entry[0]):
        pl.semaphore_signal(barrier, inc=1, device_id=device, device_id_type=MESH)

    load_panel = pltpu.make_async_copy(panel_ref, panel, load_sem.at[0])
    load_trail = pltpu.make_async_copy(trail_ref, trail, load_sem.at[1])
    load_panel.start()
    load_trail.start()

    def copy(src, dst, send_sem, recv_sem, device):
        pltpu.make_async_remote_copy(
            src_ref=src, dst_ref=dst, send_sem=send_sem, recv_sem=recv_sem,
            device_id=device, device_id_type=MESH,
        ).start()

    def scatter(k):
        for slot, (target, device) in enumerate(around):
            copy(
                send.at[k, lax.div(target, NC), lax.rem(target, NC)], rs_in.at[k, slot],
                rs_send.at[k], rs_recv.at[k], device,
            )

    def scattered(k):
        pltpu.make_async_copy(rs_in.at[k], rs_in.at[k], rs_recv.at[k]).wait()
        return [send[k, lax.div(share, NC), lax.rem(share, NC)]] + [rs_in[k, n] for n in range(SHARES - 1)]

    def exchange(k, block):
        z_out[k] = block
        for device in along:
            copy(z_out.at[k], z_in.at[k, z], z_send.at[k], z_recv.at[k], device)
        z_in[k, z] = block

    def exchanged(k):
        others = z_in.at[k, pl.ds(0, nz - 1)]
        pltpu.make_async_copy(others, others, z_recv.at[k]).wait()
        return [z_in[k, n] for n in range(nz)]

    def gather(k, block):
        gathered[k, share] = block
        for _, device in around:
            copy(
                gathered.at[k, share], gathered.at[k, share],
                ag_send.at[k], ag_recv.at[k], device,
            )

    def gathered_pair(k):
        others = gathered.at[k, pl.ds(0, SHARES - 1)]
        pltpu.make_async_copy(others, others, ag_recv.at[k]).wait()
        blocks = gathered[k].reshape(SHARES // NC, NC, TILE, ORDER)
        return unhalve(blocks[:, 0], blocks[:, 1])

    def stage(k, left, right):
        even, odd = halves(left, right)
        send[k, :, 0] = even
        send[k, :, 1] = odd

    load_panel.wait()
    scale = 1.0 / row_total
    parts = slices(panel[...])
    lead, second, third = gram_parts(parts)
    high, error = two_sum(lead, second)
    error = error + third
    total = high + error
    error = error - (total - high)
    stage(0, total * scale, error * scale)

    pl.semaphore_wait(barrier, len(along) + len(around))
    scatter(0)

    load_trail.wait()
    values = trail[...]
    t0 = values.astype(bf16)
    values = values - t0.astype(f32)
    t1 = values.astype(bf16)
    t2 = (values - t1.astype(f32)).astype(bf16)
    tn = ((0,), (0,))
    both = contract(parts[0], jnp.concatenate([t0, t1, t2], axis=1), tn, None)
    more = contract(parts[1], jnp.concatenate([t0, t1], axis=1), tn, None)
    last = contract(parts[2], t0, tn, None)
    cross = both[:, :TRAIL] + (
        (both[:, TRAIL : 2 * TRAIL] + more[:, :TRAIL])
        + (both[:, 2 * TRAIL :] + more[:, TRAIL:] + last)
    )
    cross = cross * scale
    stage(1, cross[:, :ORDER], cross[:, ORDER:])
    scatter(1)

    exchange(0, add_pairs(scattered(0), core))
    exchange(1, add_plain(scattered(1)))
    gather(0, add_pairs(exchanged(0), core))
    gather(1, add_plain(exchanged(1)))
    high, low = gathered_pair(0)

    first_factor, first_inverse = factor(high)
    factor_ref[...] = first_factor
    inverse_ref[...] = first_inverse
    lead, second, third = gram_parts(slices(first_factor))
    rest, error = two_sum(high, -lead)
    rest, more = two_sum(rest, -second)
    gap = rest + ((error + more) + (low - third))
    gap_ref[...] = times_close(times_close(first_inverse, gap), first_inverse, turned=True)

    left, right = gathered_pair(1)
    cross_ref[:, :ORDER] = left
    cross_ref[:, ORDER:] = right

    for k in range(2):
        pltpu.make_async_copy(rs_in.at[k], rs_in.at[k], rs_send.at[k]).wait()
        others = z_in.at[k, pl.ds(0, nz - 1)]
        pltpu.make_async_copy(others, others, z_send.at[k]).wait()
        others = gathered.at[k, pl.ds(0, SHARES - 1)]
        pltpu.make_async_copy(others, others, ag_send.at[k]).wait()


def reduced(panel, trailing, nz, row_total):
    rows = panel.shape[0]
    block = (TILE, ORDER)
    vmem = pl.BlockSpec(memory_space=pltpu.VMEM)
    dma = pltpu.SemaphoreType.DMA
    return pl.pallas_call(
        functools.partial(reduce_kernel, nz, row_total),
        out_shape=[pltpu.VMEM((ORDER, ORDER), f32)] * 3 + [pltpu.VMEM((ORDER, TRAIL), f32)],
        in_specs=[pl.BlockSpec(memory_space=pltpu.HBM)] * 2,
        out_specs=[vmem] * 4,
        scratch_shapes=[
            pltpu.VMEM((rows, ORDER), f32),
            pltpu.VMEM((rows, TRAIL), f32),
            pltpu.VMEM((2, SHARES // NC, NC) + block, f32),
            pltpu.VMEM((2, SHARES - 1) + block, f32),
            pltpu.VMEM((2,) + block, f32),
            pltpu.VMEM((2, nz) + block, f32),
            pltpu.VMEM((2, SHARES) + block, f32),
        ]
        + [dma((2,))] * 7,
        compiler_params=pltpu.CompilerParams(
            collective_id=0, has_side_effects=True, vmem_limit_bytes=62 * 2**20
        ),
        name="reduce_and_factor",
    )(panel, trailing)


def apply_kernel(
    factor_ref, inverse_ref, gap_ref, cross_ref, panel_ref, trail_ref,
    q_ref, r_ref, p_ref, u_ref,
    q_out, r_out, p_out, u_out, whole, small_sem, store_sem,
):
    nn, nt = ((1,), (0,)), ((1,), (1,))
    gap, first_factor, first_inverse = gap_ref[...], factor_ref[...], inverse_ref[...]
    rows = lax.broadcasted_iota(jnp.int32, gap.shape, 0)
    cols = lax.broadcasted_iota(jnp.int32, gap.shape, 1)
    eye = jnp.where(rows == cols, 1.0, 0.0).astype(f32)
    weight = jnp.where(rows > cols, 1.0, 0.5 * eye).astype(f32)
    small = jnp.sum(gap * gap) < 0.005

    start = contract(first_inverse, first_factor, nt)
    lower = weight * gap
    close = None
    for step in range(STEPS):
        lower = weight * (gap - times_close(lower, lower, turned=True))
        if step == 0:
            close = lower
    guess = first_inverse - times_close(close, first_inverse)
    guess = first_inverse - times_close(close, guess)
    left = start - times_close(close, start)
    left = start - times_close(close, left)
    rough = contract(guess, cross_ref[...], nn)
    turned = guess.T
    rest = (eye - left) - times_close(left, lower)
    whole[...] = turned + times_close(turned, rest, turned=True)
    p_out[...] = rough + contract(rest, rough, nn)
    r_out[...] = first_factor + times_close(lower.T, first_factor)

    @pl.when(jnp.logical_not(small))
    def _():
        second_factor, second_inverse = factor(eye + gap_ref[...])
        r_factor = contract(second_factor, factor_ref[...], nn)
        r_out[...] = r_factor
        guess = contract(second_inverse, inverse_ref[...], nn)
        inverse = guess + contract(eye - contract(guess, r_factor, nt), guess, nn)
        whole[...] = inverse.T
        p_out[...] = contract(inverse, cross_ref[...], nn)

    inverse, projection = split(whole[...]), split(p_out[...])
    size = panel_ref.shape[0] // CHUNKS
    stores = [
        pltpu.make_async_copy(r_out, r_ref, small_sem.at[0]),
        pltpu.make_async_copy(p_out, p_ref, small_sem.at[1]),
    ]
    stores[0].start()
    stores[1].start()
    for k in range(CHUNKS):
        part = pl.ds(k * size, size)
        q_factor = times_square(split(panel_ref[part]), inverse)
        q_out[part] = q_factor
        stores.append(pltpu.make_async_copy(q_out.at[part], q_ref.at[part], store_sem.at[0, k]))
        stores[-1].start()
        u_out[part] = trail_ref[part] - times_wide(split(q_factor), projection)
        stores.append(pltpu.make_async_copy(u_out.at[part], u_ref.at[part], store_sem.at[1, k]))
        stores[-1].start()
    for store in stores:
        store.wait()


def applied(first_factor, first_inverse, gap, cross, panel, trailing):
    rows = panel.shape[0]
    vmem = pl.BlockSpec(memory_space=pltpu.VMEM)
    hbm = pl.BlockSpec(memory_space=pltpu.HBM)
    dma = pltpu.SemaphoreType.DMA
    return pl.pallas_call(
        apply_kernel,
        out_shape=[
            jax.ShapeDtypeStruct((rows, ORDER), f32),
            jax.ShapeDtypeStruct((ORDER, ORDER), f32),
            jax.ShapeDtypeStruct((ORDER, TRAIL), f32),
            jax.ShapeDtypeStruct((rows, TRAIL), f32),
        ],
        in_specs=[vmem] * 6,
        out_specs=[hbm] * 4,
        scratch_shapes=[
            pltpu.VMEM((rows, ORDER), f32),
            pltpu.VMEM((ORDER, ORDER), f32),
            pltpu.VMEM((ORDER, TRAIL), f32),
            pltpu.VMEM((rows, TRAIL), f32),
            pltpu.VMEM((ORDER, ORDER), f32),
            dma((2,)),
            dma((2, CHUNKS)),
        ],
        compiler_params=pltpu.CompilerParams(vmem_limit_bytes=32 * 2**20),
        name="apply_factor",
    )(first_factor, first_inverse, gap, cross, panel, trailing)


def solution(mesh):
    nz = mesh.shape["wide"] // (NY * NC)

    def on_device(panel, trailing):
        row_total = float(panel.shape[0] * mesh.size)
        parts = reduced(panel, trailing, nz, row_total)
        q_factor, r_factor, projection, updated = applied(*parts, panel, trailing)
        return q_factor, r_factor, projection, updated

    rows = P(("wide", "narrow"), None)
    return jax.shard_map(
        on_device, mesh=mesh, in_specs=(rows, rows), out_specs=(rows, P(), P(), rows),
        check_vma=False,
    )
```
